256 devices in a mesh: dp: 16 (over z, core), seq: 16 (over y, x).
Axes of the slice: x: 4, y: 4, z: 8, core: 2. Of those that a mesh axis runs over, the one named last changes fastest.
Arguments:
- resid: bfloat16 [16, 2048, 1536], P('dp', 'seq'), may hold values from -6 to 6
- query: bfloat16 [16, 2048, 1024], P('dp', 'seq'), may hold values from -30 to 30
- key: bfloat16 [16, 2048, 1024], P('dp', 'seq'), may hold values from -30 to 30
- value: bfloat16 [16, 2048, 1024], P('dp', 'seq'), may hold values from -6 to 6
- out_weight: bfloat16 [1024, 1536], replicated, may hold values from -0.1875 to 0.1875
- conv_kernel: float32 [31, 1536], replicated, may hold values from -1 to 1
- conv_gain: float32 [1536], replicated, may hold values from 0.1 to 1.9
- recording_ids: int32 [16, 2048], P('dp', 'seq'), may hold values from 0 to 5, never falling along the last dimension, each value on 1 to 1024 neighbouring positions
- cotangent: bfloat16 [16, 2048, 1536], P('dp', 'seq'), may hold values from -6 to 6
Outputs:
- layer_out: bfloat16 [16, 2048, 1536], P('dp', 'seq')
- grad_resid: bfloat16 [16, 2048, 1536], P('dp', 'seq')
- grad_query: bfloat16 [16, 2048, 1024], P('dp', 'seq')
- grad_key: bfloat16 [16, 2048, 1024], P('dp', 'seq')
- grad_value: bfloat16 [16, 2048, 1024], P('dp', 'seq')
- grad_out_weight: float32 [1024, 1536], P(('dp', 'seq'))
- grad_kernel: float32 [31, 1536], replicated
- grad_gain: float32 [1536], replicated
The draws below stay inside these ranges and needn't reach their ends.
Inputs may be any that keep to these rules, and one draw needn't show every extreme that they name: `recording_ids`: recording ids never fall along a sequence; each of the 6 recordings occupies 1 to 1024 consecutive frames, one of them exactly 1024.
All inputs are finite; a program needn't handle non-finite values.
Results may differ from the reference program's by a relative error of at most 0.034.
Values may be sent and summed in bfloat16 or wider, within the bound.
A program may use at most 192 MiB of HBM per device.

```python
import math
import jax
import jax.numpy as jnp
import numpy as np
from jax import lax

D = 1536
HEADS = 16
HEAD = 64
TAPS = 31
RECS = 6
LEN = 2048
SEQS = 16
MOST = 1024


def common_rows(key):
    return jnp.clip(jax.random.normal(key, (SEQS, LEN, HEADS * HEAD), jnp.float32), -6.0, 6.0)


def draw_query(key, part):
    shared = common_rows(key)
    key = jax.random.fold_in(key, 7)
    return jnp.clip(jax.random.normal(key, shared.shape, jnp.float32), -6.0, 6.0).astype(jnp.bfloat16)


def draw_key(key, part):
    shared = common_rows(key)
    return shared.astype(jnp.bfloat16)


def steps_of(rng, dims, cuts, smallest, high):
    loudness, own = 1.0, jax.random.fold_in(rng, 6)
    for axis_at, blocks in cuts:
        steps = jnp.exp(jax.random.uniform(jax.random.fold_in(own, axis_at), (blocks,), jnp.float32, smallest / len(cuts), high / len(cuts)))
        loudness = loudness * jnp.repeat(steps, dims[axis_at] // blocks).reshape([-1 if axis == axis_at else 1 for axis in range(len(dims))])
    return loudness


def length_profile(count, total, limit, skew):
    weights = [(1 << 20) // math.isqrt(standing ** skew) + 1 for standing in range(2, count + 1)]
    surplus, given = total - limit - (count - 1), [1] * (count - 1)
    while surplus > 0:
        movable = [i for i in range(count - 1) if given[i] < limit]
        whole, left = sum([weights[i] for i in movable]), surplus
        for i in movable:
            addition = min(limit - given[i], max(1, left * weights[i] // whole), surplus)
            given[i] = given[i] + addition
            surplus = surplus - addition
    return np.array([limit] + given)


def ragged(key, number_of, total, bound, lean):
    if number_of == 2:
        one = jax.random.randint(key, (), max(1, total - bound), min(bound, total - 1) + 1)
        return jnp.stack([one, total - one])
    lengths = jnp.asarray(length_profile(number_of, total, bound, lean), jnp.int32)
    twos = (number_of - 1) // 2
    source_of, receiver = lengths[1:1 + 2 * twos:2], lengths[2:2 + 2 * twos:2]
    slack = jnp.minimum(source_of - 1, bound - receiver)
    passed = jax.random.randint(jax.random.fold_in(key, 1), (twos,), 0, 1 << 20) % (slack + 1)
    lengths = lengths.at[1:1 + 2 * twos:2].set(source_of - passed).at[2:2 + 2 * twos:2].set(receiver + passed)
    return lengths[jax.random.permutation(jax.random.fold_in(key, 2), number_of)]


def normal_values(key, extent, spread, most, pieces=(), held_as=jnp.bfloat16):
    level = steps_of(key, extent, pieces, -0.22, 0.18) if pieces else 1.0
    result = jax.random.normal(key, extent, jnp.float32) * spread * level
    return jnp.minimum(jnp.maximum(result, -most), most).astype(held_as)


def setup_inputs(seed: int = 0) -> dict:
    key_list = jax.random.split(jax.random.key(seed), 10)
    return {
        "resid": normal_values(key_list[0], (SEQS, LEN, D), 1.0, 6.0, ((0, 16), (1, 16))),
        "query": draw_query(jax.random.fold_in(key_list[9], 71), 0),
        "key": draw_key(jax.random.fold_in(key_list[9], 71), 0),
        "value": normal_values(key_list[3], (SEQS, LEN, HEADS * HEAD), 1.0, 6.0, ((0, 16), (1, 16))),
        "out_weight": normal_values(key_list[4], (HEADS * HEAD, D), (HEADS * HEAD) ** -0.5, 0.1875),
        "conv_kernel": normal_values(key_list[5], (TAPS, D), TAPS ** -0.5, 1.0, (), jnp.float32),
        "conv_gain": jnp.clip(1.0 + 0.18 * jax.random.normal(key_list[6], (D,), jnp.float32), 0.1, 1.9),
        "recording_ids": jax.vmap(lambda own: jnp.searchsorted(jnp.cumsum(ragged(own, RECS, LEN, MOST, 2)), jnp.arange(LEN), side="right"))(jax.random.split(key_list[7], SEQS)).reshape((SEQS, LEN)).astype(jnp.int32),
        "cotangent": normal_values(key_list[8], (SEQS, LEN, D), 1.0, 6.0, ((0, 16), (1, 16))),
    }


NEGATIVE = -1e+30
EPSILON = 1e-05

def head_scores(query_head, key_head, matches):
    scores = jnp.einsum('ae,be->ab', query_head.astype(jnp.float32), key_head.astype(jnp.float32)) * HEAD ** (-0.5)
    return jnp.where(matches, scores, NEGATIVE)

def weights_of(scores, matches):
    row_max = lax.optimization_barrier(jnp.max(scores, axis=-1, keepdims=True))
    unnormed = jnp.where(matches, jnp.exp(scores - row_max), 0.0)
    row_sum = lax.optimization_barrier(jnp.sum(unnormed, axis=-1, keepdims=True))
    return (unnormed / row_sum).astype(jnp.bfloat16)

def split_heads(rows):
    return rows.reshape(LEN, HEADS, HEAD).transpose(1, 0, 2)

def join_heads(blocks):
    return blocks.transpose(1, 0, 2).reshape(LEN, HEADS * HEAD)

def one_sequence(inputs, out_weight, conv_kernel, conv_gain):
    resid, query, key, value, rec_ids, cotangent = inputs
    matches = rec_ids[:, None] == rec_ids[None, :]
    margin = TAPS // 2
    heads_q = split_heads(query)
    heads_k = split_heads(key)
    heads_v = split_heads(value)

    def forward(parts):
        query_head, key_head, value_head = parts
        weights = weights_of(head_scores(query_head, key_head, matches), matches)
        return jnp.einsum('ab,be->ae', weights.astype(jnp.float32), value_head.astype(jnp.float32)).astype(jnp.bfloat16)
    heads_o = lax.map(forward, (heads_q, heads_k, heads_v))
    attn = join_heads(heads_o)
    stream = resid.astype(jnp.float32) + jnp.dot(attn, out_weight, preferred_element_type=jnp.float32)
    norm_factor = lax.rsqrt(lax.optimization_barrier(jnp.mean(stream * stream, axis=-1, keepdims=True)) + EPSILON)
    normed = stream * norm_factor
    shaped = (normed * conv_gain).astype(jnp.bfloat16)
    shaped_pad = jnp.pad(shaped, ((margin, margin), (0, 0)))
    ids_pad = jnp.pad(rec_ids, (margin, margin), constant_values=-1)
    conv = jnp.zeros((LEN, D), jnp.float32)
    for position in range(TAPS):
        match_fore = (ids_pad[position:position + LEN] == rec_ids)[:, None]
        conv = conv + jnp.where(match_fore, conv_kernel[position] * shaped_pad[position:position + LEN], 0.0)
    layer_out = (stream + jax.nn.silu(conv)).astype(jnp.bfloat16)
    sigma = jax.nn.sigmoid(conv)
    grad_conv = (cotangent.astype(jnp.float32) * sigma * (1.0 + conv * (1.0 - sigma))).astype(jnp.bfloat16)
    grad_pad = jnp.pad(grad_conv, ((margin, margin), (0, 0)))
    grad_shaped = jnp.zeros((LEN, D), jnp.float32)
    kernel_rows = []
    for position in range(TAPS):
        mirror = 2 * margin - position
        match_back = (ids_pad[mirror:mirror + LEN] == rec_ids)[:, None]
        grad_shaped = grad_shaped + jnp.where(match_back, conv_kernel[position] * grad_pad[mirror:mirror + LEN], 0.0)
        match_fore = (ids_pad[position:position + LEN] == rec_ids)[:, None]
        kernel_rows.append(lax.optimization_barrier(jnp.sum(jnp.where(match_fore, grad_conv.astype(jnp.float32) * shaped_pad[position:position + LEN].astype(jnp.float32), 0.0), axis=0)))
    grad_kernel = jnp.stack(kernel_rows)
    grad_gain = lax.optimization_barrier(jnp.sum(grad_shaped * normed, axis=0))
    scaled = grad_shaped * conv_gain
    grad_stream = cotangent.astype(jnp.float32) + norm_factor * (scaled - normed * lax.optimization_barrier(jnp.mean(scaled * normed, axis=-1, keepdims=True)))
    grad_resid = grad_stream.astype(jnp.bfloat16)
    grad_attn = jnp.dot(grad_resid, out_weight.T, preferred_element_type=jnp.float32).astype(jnp.bfloat16)
    grad_weight = jnp.dot(attn.T, grad_resid, preferred_element_type=jnp.float32)
    heads_d = split_heads(grad_attn)
    scale = HEAD ** (-0.5)

    def backward(parts):
        query_head, key_head, value_head, out_head, grad_head = parts
        weights = weights_of(head_scores(query_head, key_head, matches), matches)
        grad_f = grad_head.astype(jnp.float32)
        grad_v = jnp.einsum('ab,ae->be', weights.astype(jnp.float32), grad_f)
        drift = jnp.einsum('ae,be->ab', grad_f, value_head.astype(jnp.float32))
        row_dot = lax.optimization_barrier(jnp.sum(grad_f * out_head.astype(jnp.float32), axis=-1, keepdims=True))
        slope = (weights.astype(jnp.float32) * (drift - row_dot)).astype(jnp.bfloat16)
        grad_q = (jnp.einsum('ab,be->ae', slope.astype(jnp.float32), key_head.astype(jnp.float32)) * scale).astype(jnp.bfloat16)
        grad_k = (jnp.einsum('ab,ae->be', slope.astype(jnp.float32), query_head.astype(jnp.float32)) * scale).astype(jnp.bfloat16)
        return (grad_q, grad_k, grad_v.astype(jnp.bfloat16))
    grad_q, grad_k, grad_v = lax.map(backward, (heads_q, heads_k, heads_v, heads_o, heads_d))
    return (layer_out, grad_resid, join_heads(grad_q), join_heads(grad_k), join_heads(grad_v), grad_weight, grad_kernel, grad_gain)

def reference(resid, query, key, value, out_weight, conv_kernel, conv_gain, recording_ids, cotangent):

    def runner(inputs):
        return one_sequence(inputs, out_weight, conv_kernel, conv_gain)
    results = lax.map(runner, (resid, query, key, value, recording_ids, cotangent))
    return (results[0], results[1], results[2], results[3], results[4], lax.optimization_barrier(jnp.sum(results[5], axis=0)), lax.optimization_barrier(jnp.sum(results[6], axis=0)), lax.optimization_barrier(jnp.sum(results[7], axis=0)))
```

```python
import jax
import jax.numpy as jnp
from jax import lax
from jax.experimental import pallas as pl
from jax.experimental.pallas import tpu as pltpu
from jax.sharding import PartitionSpec as P

EPSILON = 1e-05
N = 16
F = 128
L = 2048
BIG = 1024
H = 64
A = 1024
D = 1536
TAPS = 31
EDGE = 16
TILE = 256
MESH = pl.DeviceIdType.MESH
f32, bf16, i32 = jnp.float32, jnp.bfloat16, jnp.int32


def rem(value, size):
    return lax.rem(value, size)


def loop(low, high, body):
    def step(i, carry):
        body(i)
        return carry

    lax.fori_loop(low, high, step, 0)


def times(value, size):
    return pl.multiple_of(value * size, size)


def dot(a, b, dims):
    return lax.dot_general(a, b, (dims, ((), ())), preferred_element_type=f32)


NT = ((1,), (1,))
NN = ((1,), (0,))
TN = ((0,), (0,))


class Exchange:
    def __init__(self, axis, me, send, recv, sems):
        self.axis, self.me, self.send, self.recv, self.sems = axis, me, send, recv, sems

    def copy(self, to, slot):
        return pltpu.make_async_remote_copy(
            src_ref=self.send(to),
            dst_ref=self.recv(slot),
            send_sem=self.sems.at[0, to],
            recv_sem=self.sems.at[1, slot],
            device_id={self.axis: to},
            device_id_type=MESH,
        )

    def start_to(self, to):
        self.copy(to, self.me).start()

    def start(self):
        loop(1, N, lambda k: self.start_to(rem(self.me + k, N)))

    def wait_recv(self):
        def one(k):
            source = rem(self.me + k, N)
            self.copy(source, source).wait_recv()

        loop(1, N, one)

    def wait_send(self):
        def one(k):
            to = rem(self.me + k, N)
            self.copy(to, self.me).wait_send()

        loop(1, N, one)


def kernel(
    q_ref, k_ref, v_ref, ids_ref, taps_ref, gain_ref, resid_hbm, cot_hbm, w_hbm,
    layer_ref, gresid_ref, dq_ref, dk_ref, dv_ref, wgrad_ref, ktaps_ref, ggain_ref,
    send1, recv1, ids_all, rot_qk, rot_v, qr, kr, vr, probs, out_rot, send2, recv2, attn,
    w_ref, resid_ref, cot_ref, stream, normed, pad, gpad, gshaped, gres, near_next, near_prev,
    edge_send, edge_recv, send3, recv3, rot_g, gr, dq_acc, dk_acc, dv_acc,
    two, own, core_send, core_recv, ring_send, ring_recv, total, part_send, part_recv,
    kpart, krecv, ksum, krecv2, kall,
    local_sem, sem1, sem_ids, sem2, sem3, sem4, edge_sem, core_sem, ring_sem, part_sem, ksem1, ksem2, ksem3,
):
    me, dp = lax.axis_index("seq"), lax.axis_index("dp")
    core, z = rem(dp, 2), dp // 2
    right, left = rem(me + 1, N), rem(me + N - 1, N)
    loads = [
        pltpu.make_async_copy(source, target, local_sem.at[i])
        for i, (source, target) in enumerate(
            ((w_hbm, w_ref), (resid_hbm, resid_ref), (cot_hbm, cot_ref))
        )
    ]
    for load in loads:
        load.start()

    barrier = pltpu.get_barrier_semaphore()

    def greet(k):
        pl.semaphore_signal(barrier, inc=1, device_id={"seq": rem(me + k, N)}, device_id_type=MESH)
        pl.semaphore_signal(barrier, inc=1, device_id={"dp": rem(dp + k, N)}, device_id_type=MESH)

    loop(1, N, greet)

    def pack_qkv(j):
        columns = pl.ds(times(j, 128), 128)
        qp, kp, vp = q_ref[:, columns], k_ref[:, columns], v_ref[:, columns]
        for half in range(2):
            c = slice(64 * half, 64 * half + 64)
            send1[2 * j + half, 0:F, :] = jnp.concatenate([qp[:, c], kp[:, c]], axis=1)
            send1[2 * j + half, F : F + 64, :] = jnp.concatenate([vp[0:64, c], vp[64:128, c]], axis=1)

    loop(0, N // 2, pack_qkv)
    ids_all[me] = jnp.broadcast_to(ids_ref[...], (8, F))
    pl.semaphore_wait(barrier, 2 * (N - 1))

    give_ids = Exchange("seq", me, lambda to: ids_all.at[me], lambda s: ids_all.at[s], sem_ids)
    give_qkv = Exchange("seq", me, lambda to: send1.at[to], lambda s: recv1.at[s], sem1)
    give_ids.start()
    give_qkv.start()
    recv1[me] = send1[me]
    give_ids.wait_recv()

    ids = ids_all[...]
    bounds = [jnp.int32(0)]
    for u in range(1, 6):
        bounds.append(jnp.sum(jnp.where(ids < u, 1, 0)) // 8)
    bounds.append(jnp.int32(L))
    start = jnp.int32(0)
    for u in range(6):
        start = start + jnp.where(bounds[u + 1] - bounds[u] == BIG, bounds[u], 0)
    marks = [(bounds[u] - start - BIG) & (L - 1) for u in range(6)]

    frame = me * F + lax.broadcasted_iota(i32, (F, 128), 0)
    low, high = jnp.zeros((F, 128), i32), jnp.full((F, 128), L, i32)
    for u in range(1, 6):
        low = jnp.maximum(low, jnp.where(bounds[u] <= frame, bounds[u], 0))
        high = jnp.minimum(high, jnp.where(bounds[u] > frame, bounds[u], L))
    near_next[...] = high - frame
    near_prev[...] = frame - low

    give_qkv.wait_recv()

    def widen(i):
        rot_qk[pl.ds(times(i, F), F), :] = recv1[i, 0:F, :].astype(f32)
        values = recv1[i, F : F + 64, :].astype(f32)
        rot_v[pl.ds(times(i, F), 64), :] = values[:, :64]
        rot_v[pl.ds(pl.multiple_of(i * F + 64, 64), 64), :] = values[:, 64:]

    loop(0, N, widen)
    rot_qk[L : L + F, :] = rot_qk[0:F, :]
    rot_v[L : L + F, :] = rot_v[0:F, :]

    def turn(i):
        at = (start + i * F) & (L - 1)
        rows = pl.ds(times(i, F), F)
        both = rot_qk[pl.ds(at, F), :]
        qr[rows, :] = (both[:, :64] * H**-0.5).astype(bf16)
        kr[rows, :] = both[:, 64:].astype(bf16)
        vr[rows, :] = rot_v[pl.ds(at, F), :].astype(bf16)

    loop(0, N, turn)

    column = lax.broadcasted_iota(i32, (1, BIG), 1)
    column_part = jnp.zeros((1, BIG), i32)
    for mark in marks:
        column_part = column_part + jnp.where(column >= mark, 1, 0)

    def attend(base, masked):
        def tile(t):
            rows = pl.ds(pl.multiple_of(base + t * TILE, TILE), TILE)
            scores = dot(qr[rows, :], kr[base : base + BIG, :], NT)
            if masked:
                row = t * TILE + lax.broadcasted_iota(i32, (TILE, 1), 0)
                row_part = jnp.zeros((TILE, 1), i32)
                for mark in marks:
                    row_part = row_part + jnp.where(row >= mark, 1, 0)
                scores = jnp.where(row_part == column_part, scores, -1e30)
            unnormed = jnp.exp(scores - jnp.max(scores, axis=1, keepdims=True))
            weights = (unnormed * (1.0 / jnp.sum(unnormed, axis=1, keepdims=True))).astype(bf16)
            probs[rows, :] = weights
            out_rot[rows, :] = dot(weights, vr[base : base + BIG, :], NN).astype(bf16).astype(f32)

        loop(0, BIG // TILE, tile)

    attend(0, False)
    attend(BIG, True)
    out_rot[L : L + F, :] = out_rot[0:F, :]

    give_out = Exchange("seq", me, lambda to: send2.at[to], lambda s: recv2.at[s], sem2)

    def pack_out(i):
        part = out_rot[pl.ds((i * F - start) & (L - 1), F), :]
        send2[i] = jnp.concatenate([part[0:64, :], part[64:128, :]], axis=1).astype(bf16)

    def send_out(k):
        to = rem(me + k, N)
        pack_out(to)
        give_out.start_to(to)

    loop(1, N, send_out)
    pack_out(me)
    recv2[me] = send2[me]
    give_out.wait_recv()

    def join(j):
        a, b = recv2[2 * j], recv2[2 * j + 1]
        columns = pl.ds(times(j, 128), 128)
        attn[0:64, columns] = jnp.concatenate([a[:, :64], b[:, :64]], axis=1)
        attn[64:128, columns] = jnp.concatenate([a[:, 64:], b[:, 64:]], axis=1)

    loop(0, N // 2, join)

    for load in loads:
        load.wait()

    def fold(value):
        return sum(value[:, 128 * c : 128 * c + 128] for c in range(value.shape[1] // 128))

    def project(c, squares):
        columns = pl.ds(times(c, 256), 256)
        part = resid_ref[:, columns].astype(f32) + dot(attn[...], w_ref[:, columns], NN)
        stream[:, columns] = part
        return squares + fold(part * part)

    squares = lax.fori_loop(0, D // 256, project, jnp.zeros((F, 128), f32))
    factor = lax.rsqrt(jnp.sum(squares, axis=1, keepdims=True) * (1.0 / D) + EPSILON)

    def norm(c):
        columns = pl.ds(times(c, 256), 256)
        part = stream[:, columns] * factor
        normed[:, columns] = part
        shaped = (part * gain_ref[:, columns]).astype(bf16)
        pad[EDGE : EDGE + F, columns] = shaped.astype(f32)
        edge_send[0, :, columns] = shaped[0:EDGE, :]
        edge_send[1, :, columns] = shaped[F - EDGE : F, :]

    loop(0, D // 256, norm)

    def edges(turn_of):
        def copy(side, to):
            return pltpu.make_async_remote_copy(
                src_ref=edge_send.at[2 * turn_of + side],
                dst_ref=edge_recv.at[2 * turn_of + side],
                send_sem=edge_sem.at[0, 2 * turn_of + side],
                recv_sem=edge_sem.at[1, 2 * turn_of + side],
                device_id={"seq": to},
                device_id_type=MESH,
            )

        return copy(0, left), copy(1, right)

    halo = edges(0)
    for copy in halo:
        copy.start()
    for copy in halo:
        copy.wait_recv()
    pad[EDGE + F :, :] = edge_recv[0].astype(f32)
    pad[0:EDGE, :] = edge_recv[1].astype(f32)

    def inside(step):
        if step > 0:
            return near_next[...] > step
        return near_prev[...] >= -step

    def convolve(c):
        columns = pl.ds(times(c, 128), 128)
        conv = jnp.zeros((F, 128), f32)
        for i in range(TAPS):
            step = i - TAPS // 2
            part = taps_ref[i : i + 1, columns] * pad[EDGE + step : EDGE + step + F, columns]
            conv = conv + (jnp.where(inside(step), part, 0.0) if step else part)
        sigma = 1.0 / (1.0 + jnp.exp(-conv))
        layer_ref[:, columns] = (stream[:, columns] + conv * sigma).astype(bf16)
        grad = cot_ref[:, columns].astype(f32) * sigma * (1.0 + conv * (1.0 - sigma))
        grad = grad.astype(bf16)
        gpad[EDGE : EDGE + F, columns] = grad.astype(f32)
        edge_send[2, :, columns] = grad[0:EDGE, :]
        edge_send[3, :, columns] = grad[F - EDGE : F, :]

    loop(0, D // 128, convolve)
    grad_halo = edges(1)
    for copy in grad_halo:
        copy.start()

    def kernel_rows(c):
        columns = pl.ds(times(c, 128), 128)
        grad = gpad[EDGE : EDGE + F, columns]
        for i in range(TAPS):
            step = i - TAPS // 2
            part = grad * pad[EDGE + step : EDGE + step + F, columns]
            if step:
                part = jnp.where(inside(step), part, 0.0)
            kpart[pl.ds(c * 32 + i, 1), :] = jnp.sum(part, axis=0, keepdims=True)

    loop(0, D // 128, kernel_rows)
    for copy in grad_halo:
        copy.wait_recv()
    gpad[EDGE + F :, :] = edge_recv[2].astype(f32)
    gpad[0:EDGE, :] = edge_recv[3].astype(f32)

    def convolve_back(c, dots):
        columns = pl.ds(times(c, 128), 128)
        grad = jnp.zeros((F, 128), f32)
        for i in range(TAPS):
            step = TAPS // 2 - i
            part = taps_ref[i : i + 1, columns] * gpad[EDGE + step : EDGE + step + F, columns]
            grad = grad + (jnp.where(inside(step), part, 0.0) if step else part)
        unit = normed[:, columns]
        kpart[pl.ds(c * 32 + TAPS, 1), :] = jnp.sum(grad * unit, axis=0, keepdims=True)
        scaled = grad * gain_ref[:, columns]
        gshaped[:, columns] = scaled
        return dots + scaled * unit

    dots = lax.fori_loop(0, D // 128, convolve_back, jnp.zeros((F, 128), f32))
    mean = jnp.sum(dots, axis=1, keepdims=True) * (1.0 / D)

    def kpiece(s):
        return pl.ds(pl.multiple_of(s * 24, 8), 24)

    ksum1 = Exchange("seq", me, lambda to: kpart.at[kpiece(to)], lambda s: krecv.at[s], ksem1)
    ksum1.start()

    def into_stream(c):
        columns = pl.ds(times(c, 256), 256)
        part = gshaped[:, columns] - normed[:, columns] * mean
        grad = (cot_ref[:, columns].astype(f32) + factor * part).astype(bf16)
        gres[:, columns] = grad
        gresid_ref[:, columns] = grad

    loop(0, D // 256, into_stream)

    give_grad = Exchange("seq", me, lambda to: send3.at[to], lambda s: recv3.at[s], sem3)

    def into_attn(j):
        grad = dot(gres[...], w_ref[pl.ds(times(j, 256), 256), :], NT).astype(bf16)
        for part in range(4):
            c = slice(64 * part, 64 * part + 64)
            send3[4 * j + part] = jnp.concatenate([grad[0:64, c], grad[64:128, c]], axis=1)

    loop(0, N // 4, into_attn)
    give_grad.start()
    recv3[me] = send3[me]

    def core_copy(j):
        return pltpu.make_async_remote_copy(
            src_ref=core_send.at[j],
            dst_ref=core_recv.at[j],
            send_sem=core_sem.at[0, j],
            recv_sem=core_sem.at[1, j],
            device_id={"dp": dp + 1 - 2 * core},
            device_id_type=MESH,
        )

    def project_grad(j):
        for c in range(D // 512):
            columns = slice(512 * c, 512 * c + 512)
            grad = dot(attn[:, pl.ds(times(j, 128), 128)], gres[:, columns], TN)
            two[0, :, columns] = grad[0:64, :]
            two[1, :, columns] = grad[64:128, :]
        own[j] = two[core]
        core_send[j] = two[1 - core].astype(bf16)
        core_copy(j).start()

    loop(0, N // 2, project_grad)

    ksum1.wait_recv()
    krecv[me] = kpart[kpiece(me), :]

    def add_up(ref):
        value = ref[0]
        for i in range(1, N):
            value = value + ref[i]
        return value

    ksum[...] = add_up(krecv)
    ksum2 = Exchange("dp", dp, lambda to: ksum, lambda s: krecv2.at[s], ksem2)
    ksum2.start()
    krecv2[dp] = ksum[...]

    give_grad.wait_recv()

    def widen_grad(i):
        values = recv3[i].astype(f32)
        rot_g[pl.ds(times(i, F), 64), :] = values[:, :64]
        rot_g[pl.ds(pl.multiple_of(i * F + 64, 64), 64), :] = values[:, 64:]

    loop(0, N, widen_grad)
    rot_g[L : L + F, :] = rot_g[0:F, :]

    def turn_grad(i):
        gr[pl.ds(times(i, F), F), :] = rot_g[pl.ds((start + i * F) & (L - 1), F), :].astype(bf16)

    loop(0, N, turn_grad)

    loop(0, N // 2, lambda j: core_copy(j).wait_recv())

    def ring_copy(way, s):
        return pltpu.make_async_remote_copy(
            src_ref=ring_send.at[way, s],
            dst_ref=ring_recv.at[way, s],
            send_sem=ring_sem.at[0, way, s],
            recv_sem=ring_sem.at[1, way, s],
            device_id={"dp": rem(dp + (2 if way == 0 else N - 2), N)},
            device_id_type=MESH,
        )

    half = D // 2

    def ring_step(s):
        for way in range(2):
            block = rem(z + 15 - s, 8) if way == 0 else rem(z + 1 + s, 8)
            columns = slice(half * way, half * way + half)
            value = own[block, :, columns] + core_recv[block, :, columns].astype(f32)
            ring_send[way, s] = value.astype(bf16)

            @pl.when(s > 0)
            def _():
                ring_copy(way, s - 1).wait_recv()
                ring_send[way, s] = (value + ring_recv[way, s - 1].astype(f32)).astype(bf16)

            ring_copy(way, s).start()

    dk_acc[...] = jnp.zeros((L, H), f32)
    dv_acc[...] = jnp.zeros((L, H), f32)

    def back(t):
        @pl.when(t < 7)
        def _():
            ring_step(t)

        rows = pl.ds(times(t, TILE), TILE)
        keys = pl.ds(times(t // (BIG // TILE), BIG), BIG)
        grad, weights = gr[rows, :], probs[rows, :]
        drift = dot(grad, vr[keys, :], NT)
        row_dot = jnp.sum(grad.astype(f32) * out_rot[rows, :], axis=1, keepdims=True)
        slope = (weights.astype(f32) * (drift - row_dot)).astype(bf16)
        dq_acc[rows, :] = dot(slope, kr[keys, :], NN) * H**-0.5
        dk_acc[keys, :] += dot(slope, qr[rows, :], TN)
        dv_acc[keys, :] += dot(weights, grad, TN)

    loop(0, L // TILE, back)

    give_qkv.wait_send()
    rot_qk[0:L, :] = jnp.concatenate([dq_acc[...], dk_acc[...]], axis=1)
    rot_v[0:L, :] = dv_acc[...]
    rot_qk[L : L + F, :] = rot_qk[0:F, :]
    rot_v[L : L + F, :] = rot_v[0:F, :]
    give_back = Exchange("seq", me, lambda to: send1.at[to], lambda s: recv4.at[s], sem4)
    recv4 = recv1

    def pack_back(i):
        at = (i * F - start) & (L - 1)
        send1[i, 0:F, :] = rot_qk[pl.ds(at, F), :].astype(bf16)
        part = rot_v[pl.ds(at, F), :]
        send1[i, F : F + 64, :] = jnp.concatenate([part[0:64, :], part[64:128, :]], axis=1).astype(bf16)

    def send_back(k):
        to = rem(me + k, N)
        pack_back(to)
        give_back.start_to(to)

    loop(1, N, send_back)
    pack_back(me)
    recv4[me] = send1[me]

    ksum2.wait_recv()
    kall[kpiece(me), :] = add_up(krecv2)
    ksum3 = Exchange("seq", me, lambda to: kall.at[kpiece(me)], lambda s: kall.at[kpiece(s)], ksem3)
    ksum3.start()

    value = own[z] + core_recv[z].astype(f32)
    for way in range(2):
        ring_copy(way, 6).wait_recv()
        columns = slice(half * way, half * way + half)
        total[:, columns] = value[:, columns] + ring_recv[way, 6].astype(f32)

    def pack_part(j):
        for c in range(D // 128):
            pair = total[pl.ds(times(j, 8), 8), 128 * c : 128 * c + 128]
            for k in range(2):
                two[k, 4 * c : 4 * c + 4, 0:128] = pair[4 * k : 4 * k + 4, :]
        for k in range(2):
            part_send[2 * j + k] = two[k, 0:48, 0:128].astype(bf16)

    loop(0, N // 2, pack_part)
    give_part = Exchange("seq", me, lambda to: part_send.at[to], lambda s: part_recv.at[s], part_sem)
    give_part.start()
    part_recv[me] = part_send[me]

    ksum3.wait_recv()
    for c in range(D // 128):
        columns = slice(128 * c, 128 * c + 128)
        ktaps_ref[:, columns] = kall[32 * c : 32 * c + TAPS, :]
        ggain_ref[:, columns] = kall[32 * c + TAPS : 32 * c + 32, :]

    give_back.wait_recv()

    def unpack(j):
        a, b = recv4[2 * j], recv4[2 * j + 1]
        columns = pl.ds(times(j, 128), 128)
        dq_ref[:, columns] = jnp.concatenate([a[0:F, :64], b[0:F, :64]], axis=1)
        dk_ref[:, columns] = jnp.concatenate([a[0:F, 64:], b[0:F, 64:]], axis=1)
        dv_ref[0:64, columns] = jnp.concatenate([a[F:, :64], b[F:, :64]], axis=1)
        dv_ref[64:128, columns] = jnp.concatenate([a[F:, 64:], b[F:, 64:]], axis=1)

    loop(0, N // 2, unpack)

    give_part.wait_recv()
    piece = part_recv[0].astype(f32)
    for i in range(1, N):
        piece = piece + part_recv[i].astype(f32)
    for c in range(D // 128):
        wgrad_ref[:, 128 * c : 128 * c + 128] = piece[4 * c : 4 * c + 4, :]

    for exchange in (give_ids, give_out, give_grad, give_back, ksum1, ksum2, ksum3, give_part):
        exchange.wait_send()
    for copy in halo + grad_halo:
        copy.wait_send()
    loop(0, N // 2, lambda j: core_copy(j).wait_send())

    def ring_done(s):
        for way in range(2):
            ring_copy(way, s).wait_send()

    loop(0, 7, ring_done)


def local(resid, query, key, value, out_weight, conv_kernel, conv_gain, recording_ids, cotangent):
    vmem = pl.BlockSpec(memory_space=pltpu.VMEM)
    hbm = pl.BlockSpec(memory_space=pl.ANY)
    scratch = [
        pltpu.VMEM((N, 192, 128), bf16),
        pltpu.VMEM((N, 192, 128), bf16),
        pltpu.VMEM((N, 8, 128), i32),
        pltpu.VMEM((L + F, 128), f32),
        pltpu.VMEM((L + F, H), f32),
        pltpu.VMEM((L, H), bf16),
        pltpu.VMEM((L, H), bf16),
        pltpu.VMEM((L, H), bf16),
        pltpu.VMEM((L, BIG), bf16),
        pltpu.VMEM((L + F, H), f32),
        pltpu.VMEM((N, 64, 128), bf16),
        pltpu.VMEM((N, 64, 128), bf16),
        pltpu.VMEM((F, A), bf16),
        pltpu.VMEM((A, D), bf16),
        pltpu.VMEM((F, D), bf16),
        pltpu.VMEM((F, D), bf16),
        pltpu.VMEM((F, D), f32),
        pltpu.VMEM((F, D), f32),
        pltpu.VMEM((F + 2 * EDGE, D), f32),
        pltpu.VMEM((F + 2 * EDGE, D), f32),
        pltpu.VMEM((F, D), f32),
        pltpu.VMEM((F, D), bf16),
        pltpu.VMEM((F, 128), i32),
        pltpu.VMEM((F, 128), i32),
        pltpu.VMEM((4, EDGE, D), bf16),
        pltpu.VMEM((4, EDGE, D), bf16),
        pltpu.VMEM((N, 64, 128), bf16),
        pltpu.VMEM((N, 64, 128), bf16),
        pltpu.VMEM((L + F, H), f32),
        pltpu.VMEM((L, H), bf16),
        pltpu.VMEM((L, H), f32),
        pltpu.VMEM((L, H), f32),
        pltpu.VMEM((L, H), f32),
        pltpu.VMEM((2, 64, D), f32),
        pltpu.VMEM((8, 64, D), f32),
        pltpu.VMEM((8, 64, D), bf16),
        pltpu.VMEM((8, 64, D), bf16),
        pltpu.VMEM((2, 7, 64, D // 2), bf16),
        pltpu.VMEM((2, 7, 64, D // 2), bf16),
        pltpu.VMEM((64, D), f32),
        pltpu.VMEM((N, 48, 128), bf16),
        pltpu.VMEM((N, 48, 128), bf16),
        pltpu.VMEM((384, 128), f32),
        pltpu.VMEM((N, 24, 128), f32),
        pltpu.VMEM((24, 128), f32),
        pltpu.VMEM((N, 24, 128), f32),
        pltpu.VMEM((384, 128), f32),
        pltpu.SemaphoreType.DMA((3,)),
        pltpu.SemaphoreType.DMA((2, N)),
        pltpu.SemaphoreType.DMA((2, N)),
        pltpu.SemaphoreType.DMA((2, N)),
        pltpu.SemaphoreType.DMA((2, N)),
        pltpu.SemaphoreType.DMA((2, N)),
        pltpu.SemaphoreType.DMA((2, 4)),
        pltpu.SemaphoreType.DMA((2, 8)),
        pltpu.SemaphoreType.DMA((2, 2, 7)),
        pltpu.SemaphoreType.DMA((2, N)),
        pltpu.SemaphoreType.DMA((2, N)),
        pltpu.SemaphoreType.DMA((2, N)),
        pltpu.SemaphoreType.DMA((2, N)),
    ]
    outs = pl.pallas_call(
        kernel,
        out_shape=(
            jax.ShapeDtypeStruct((F, D), bf16),
            jax.ShapeDtypeStruct((F, D), bf16),
            jax.ShapeDtypeStruct((F, A), bf16),
            jax.ShapeDtypeStruct((F, A), bf16),
            jax.ShapeDtypeStruct((F, A), bf16),
            jax.ShapeDtypeStruct((4, D), f32),
            jax.ShapeDtypeStruct((TAPS, D), f32),
            jax.ShapeDtypeStruct((1, D), f32),
        ),
        in_specs=[vmem] * 6 + [hbm] * 3,
        out_specs=(vmem,) * 8,
        scratch_shapes=scratch,
        compiler_params=pltpu.CompilerParams(
            collective_id=0, has_side_effects=True, vmem_limit_bytes=56 * 1024 * 1024
        ),
        name="conformer",
    )(
        query[0], key[0], value[0], recording_ids, conv_kernel, conv_gain[None],
        resid[0], cotangent[0], out_weight,
    )
    layer_out, grad_resid, grad_q, grad_k, grad_v, grad_w, grad_taps, grad_gain = outs
    return (
        layer_out[None], grad_resid[None], grad_q[None], grad_k[None], grad_v[None],
        grad_w, grad_taps, grad_gain[0],
    )


def solution(mesh):
    rows = P("dp", "seq", None)
    return jax.shard_map(
        local,
        mesh=mesh,
        in_specs=(rows, rows, rows, rows, P(), P(), P(), P("dp", "seq"), rows),
        out_specs=(rows, rows, rows, rows, rows, P(("dp", "seq"), None), P(), P()),
        check_vma=False,
    )
```

```python
import jax
import jax.numpy as jnp
from jax import lax
from jax.experimental import pallas as pl
from jax.experimental.pallas import tpu as pltpu
from jax.sharding import PartitionSpec as P

EPSILON = 1e-05
N = 16
F = 128
L = 2048
BIG = 1024
H = 64
A = 1024
D = 1536
TAPS = 31
EDGE = 16
TILE = 256
SPLIT = 1024
MESH = pl.DeviceIdType.MESH
f32, bf16, i32 = jnp.float32, jnp.bfloat16, jnp.int32


def rem(value, size):
    return lax.rem(value, size)


def loop(low, high, body):
    def step(i, carry):
        body(i)
        return carry

    lax.fori_loop(low, high, step, 0)


def times(value, size):
    return pl.multiple_of(value * size, size)


def dot(a, b, dims):
    return lax.dot_general(a, b, (dims, ((), ())), preferred_element_type=f32)


NT = ((1,), (1,))
NN = ((1,), (0,))
TN = ((0,), (0,))


class Copies:
    def __init__(self, flights, count, copy):
        self.count, self.copy, self.received = count, copy, False
        flights.append(self)

    def start(self, i):
        self.copy(i).start()

    def wait_recv(self):
        self.received = True
        loop(0, self.count, lambda i: self.copy(i).wait_recv())

    def wait_send(self):
        loop(0, self.count, lambda i: self.copy(i).wait_send())


class Exchange:
    def __init__(self, flights, device, count, me, send, recv, sems):
        self.device, self.count, self.me = device, count, me
        self.send, self.recv, self.sems = send, recv, sems
        self.received = False
        flights.append(self)

    def copy(self, to, slot):
        return pltpu.make_async_remote_copy(
            src_ref=self.send(to),
            dst_ref=self.recv(slot),
            send_sem=self.sems.at[0, to],
            recv_sem=self.sems.at[1, slot],
            device_id=self.device(to),
            device_id_type=MESH,
        )

    def others(self, body):
        loop(1, self.count, lambda k: body(rem(self.me + k, self.count)))

    def start_to(self, to):
        self.copy(to, self.me).start()

    def start(self):
        self.others(self.start_to)

    def wait_recv(self):
        self.received = True
        self.others(lambda source: self.copy(source, source).wait_recv())

    def wait_send(self):
        self.others(lambda to: self.copy(to, self.me).wait_send())


def kernel(
    q_hbm, k_hbm, v_hbm, ids_ref, taps_hbm, gain_in, resid_hbm, cot_hbm, w_hbm,
    layer_hbm, gresid_hbm, dq_hbm, dk_hbm, dv_hbm, wgrad_ref, ktaps_ref, ggain_ref,
    q_ref, k_ref, v_ref, taps_ref, gain_ref, layer_ref, dq_ref, dk_ref, dv_ref, shift, gshift, send0, recv0,
    send1, recv1, ids_all, rot_qk, rot_v, qr, kr, vr, probs, out_rot, send2, recv2, attn,
    w_ref, resid_ref, cot_ref, stream, normed, pad, gpad, gshaped, gres, near_next, near_prev, dots_ref,
    edge_send, edge_recv, send3, recv3, send4, recv4, rot_g, gr, kv_acc,
    two, own, core_send, core_recv, z_send, z_recv, seq_send, seq_recv, z_send2, z_recv2, seq_send2, seq_recv2,
    kpart, krecv, ksum, krecv2, kall,
    local_sem, sem0, sem1, sem_ids, sem2, sem3, sem4, edge_sem, core_sem, z_sem, seq_sem, z_sem2, seq_sem2, ksem1, ksem2, ksem3,
):
    flights = []
    me, dp = lax.axis_index("seq"), lax.axis_index("dp")
    core, z = rem(dp, 2), dp // 2
    over_seq = (lambda to: {"seq": to}), N, me
    over_dp = (lambda to: {"dp": to}), N, dp
    over_z = (lambda to: {"dp": 2 * to + core}), N // 2, z
    pairs = (
        (q_hbm, q_ref), (k_hbm, k_ref), (v_hbm, v_ref),
        (w_hbm, w_ref), (resid_hbm, resid_ref), (cot_hbm, cot_ref), (taps_hbm, taps_ref),
        (layer_ref, layer_hbm), (gres, gresid_hbm), (dq_ref, dq_hbm), (dk_ref, dk_hbm), (dv_ref, dv_hbm),
    )
    moves = [pltpu.make_async_copy(a, b, local_sem.at[i]) for i, (a, b) in enumerate(pairs)]
    first, loads, stores = moves[:3], moves[3:7], moves[7:]
    for load in first + loads:
        load.start()
    gain_ref[0, :] = gain_in[...]

    barrier = pltpu.get_barrier_semaphore()

    def greet(k):
        pl.semaphore_signal(barrier, inc=1, device_id={"seq": rem(me + k, N)}, device_id_type=MESH)
        pl.semaphore_signal(barrier, inc=1, device_id={"dp": rem(dp + k, N)}, device_id_type=MESH)

    loop(1, N, greet)

    for load in first:
        load.wait()

    def pack_qkv(j):
        columns = pl.ds(times(j, 128), 128)
        qp, kp, vp = q_ref[:, columns], k_ref[:, columns], v_ref[:, columns]
        for half in range(2):
            c = slice(64 * half, 64 * half + 64)
            send0[2 * j + half] = jnp.concatenate([qp[:, c], kp[:, c]], axis=1)
            send1[2 * j + half] = jnp.concatenate([vp[0:64, c], vp[64:128, c]], axis=1)

    loop(0, N // 2, pack_qkv)
    ids_all[me] = jnp.broadcast_to(ids_ref[...], (8, F))
    pl.semaphore_wait(barrier, 2 * (N - 1))

    give_ids = Exchange(flights, *over_seq, lambda to: ids_all.at[me], lambda s: ids_all.at[s], sem_ids)
    give_qk = Exchange(flights, *over_seq, lambda to: send0.at[to], lambda s: recv0.at[s], sem0)
    give_v = Exchange(flights, *over_seq, lambda to: send1.at[to], lambda s: recv1.at[s], sem1)
    give_ids.start()
    give_qk.start()
    give_v.start()
    recv0[me] = send0[me]
    recv1[me] = send1[me]
    give_ids.wait_recv()

    ids = ids_all[...]
    bounds = [jnp.int32(0)]
    for u in range(1, 6):
        bounds.append(jnp.sum(jnp.where(ids < u, 1, 0)) // 8)
    bounds.append(jnp.int32(L))
    start = jnp.int32(0)
    for u in range(6):
        start = start + jnp.where(bounds[u + 1] - bounds[u] == BIG, bounds[u], 0)
    marks = [(bounds[u] - start - BIG) & (L - 1) for u in range(6)]

    frame = me * F + lax.broadcasted_iota(i32, (F, 128), 0)
    low, high = jnp.zeros((F, 128), i32), jnp.full((F, 128), L, i32)
    for u in range(1, 6):
        low = jnp.maximum(low, jnp.where(bounds[u] <= frame, bounds[u], 0))
        high = jnp.minimum(high, jnp.where(bounds[u] > frame, bounds[u], L))
    near_next[...] = high - frame
    near_prev[...] = frame - low

    give_qk.wait_recv()

    def widen(i):
        rot_qk[pl.ds(times(i, F), F), :] = recv0[i].astype(f32)

    loop(0, N, widen)
    rot_qk[L : L + F, :] = rot_qk[0:F, :]

    def turn(i):
        rows = pl.ds(times(i, F), F)
        both = rot_qk[pl.ds((start + i * F) & (L - 1), F), :]
        qr[rows, :] = (both[:, :64] * H**-0.5).astype(bf16)
        kr[rows, :] = both[:, 64:].astype(bf16)

    loop(0, N, turn)

    column = lax.broadcasted_iota(i32, (1, BIG), 1)
    column_part = jnp.zeros((1, BIG), i32)
    for mark in marks:
        column_part = column_part + jnp.where(column >= mark, 1, 0)

    def weigh(base, masked):
        def tile(t):
            rows = pl.ds(pl.multiple_of(base + t * TILE, TILE), TILE)
            scores = dot(qr[rows, :], kr[base : base + BIG, :], NT)
            if masked:
                row = t * TILE + lax.broadcasted_iota(i32, (TILE, 1), 0)
                row_part = jnp.zeros((TILE, 1), i32)
                for mark in marks:
                    row_part = row_part + jnp.where(row >= mark, 1, 0)
                scores = jnp.where(row_part == column_part, scores, -1e30)
            unnormed = jnp.exp(scores - jnp.max(scores, axis=1, keepdims=True))
            probs[rows, :] = (unnormed * (1.0 / jnp.sum(unnormed, axis=1, keepdims=True))).astype(bf16)

        loop(0, BIG // TILE, tile)

    weigh(0, False)
    weigh(BIG, True)

    give_v.wait_recv()

    def widen_v(i):
        values = recv1[i].astype(f32)
        rot_v[pl.ds(times(i, F), 64), :] = values[:, :64]
        rot_v[pl.ds(pl.multiple_of(i * F + 64, 64), 64), :] = values[:, 64:]

    loop(0, N, widen_v)
    rot_v[L : L + F, :] = rot_v[0:F, :]

    def turn_v(i):
        vr[pl.ds(times(i, F), F), :] = rot_v[pl.ds((start + i * F) & (L - 1), F), :].astype(bf16)

    loop(0, N, turn_v)

    def mix(t):
        rows = pl.ds(times(t, TILE), TILE)
        keys = pl.ds(times(t // (BIG // TILE), BIG), BIG)
        out_rot[rows, :] = dot(probs[rows, :], vr[keys, :], NN).astype(bf16).astype(f32)

    loop(0, L // TILE, mix)
    out_rot[L : L + F, :] = out_rot[0:F, :]

    give_out = Exchange(flights, *over_seq, lambda to: send2.at[to], lambda s: recv2.at[s], sem2)

    def pack_out(i):
        part = out_rot[pl.ds((i * F - start) & (L - 1), F), :]
        send2[i] = jnp.concatenate([part[0:64, :], part[64:128, :]], axis=1).astype(bf16)

    def send_out(k):
        to = rem(me + k, N)
        pack_out(to)
        give_out.start_to(to)

    loop(1, N, send_out)
    pack_out(me)
    recv2[me] = send2[me]
    give_out.wait_recv()

    def join(j):
        a, b = recv2[2 * j], recv2[2 * j + 1]
        columns = pl.ds(times(j, 128), 128)
        for k, (first, second) in enumerate(((a, b), (b, a))):
            attn[k, 0:64, columns] = jnp.concatenate([first[:, :64], second[:, :64]], axis=1)
            attn[k, 64:128, columns] = jnp.concatenate([first[:, 64:], second[:, 64:]], axis=1)

    loop(0, N // 2, join)

    for load in loads:
        load.wait()

    def fold(value):
        return sum(value[:, 128 * c : 128 * c + 128] for c in range(value.shape[1] // 128))

    def project(c, squares):
        columns = pl.ds(times(c, 256), 256)
        part = resid_ref[:, columns].astype(f32) + dot(attn[0], w_ref[:, columns], NN)
        stream[:, columns] = part
        return squares + fold(part * part)

    squares = lax.fori_loop(0, D // 256, project, jnp.zeros((F, 128), f32))
    factor = lax.rsqrt(jnp.sum(squares, axis=1, keepdims=True) * (1.0 / D) + EPSILON)

    def norm(c):
        columns = pl.ds(times(c, 256), 256)
        part = stream[:, columns] * factor
        normed[:, columns] = part
        shaped = (part * gain_ref[:, columns]).astype(bf16)
        pad[EDGE : EDGE + F, columns] = shaped.astype(f32)
        edge_send[0, :, columns] = shaped[0:EDGE, :]
        edge_send[1, :, columns] = shaped[F - EDGE : F, :]

    loop(0, D // 256, norm)

    def edges(turn_of):
        def copy(side):
            return pltpu.make_async_remote_copy(
                src_ref=edge_send.at[2 * turn_of + side],
                dst_ref=edge_recv.at[2 * turn_of + side],
                send_sem=edge_sem.at[0, 2 * turn_of + side],
                recv_sem=edge_sem.at[1, 2 * turn_of + side],
                device_id={"seq": rem(me + jnp.where(side == 0, N - 1, 1), N)},
                device_id_type=MESH,
            )

        return Copies(flights, 2, copy)

    halo = edges(0)
    halo.start(0)
    halo.start(1)

    def shift_rows(source, target, low, high):
        def one(c):
            columns = pl.ds(times(c, 128), 128)
            for s in range(8):
                target[s, low:high, columns] = source[low + s + 1 : high + s + 1, columns]

        loop(0, D // 128, one)

    shift_rows(pad, shift, 16, 128)

    def inside(step, rows):
        if step > 0:
            return near_next[rows, :] > step
        return near_prev[rows, :] >= -step

    def over_taps(source, low, count, wide, first_column, mirrored):
        rows = slice(low, low + count)
        sums = [jnp.zeros((count, 128), f32)] * wide
        for i in range(TAPS):
            step = i - TAPS // 2
            mask = inside(step, rows)
            at = slice(low + i // 8 * 8, low + i // 8 * 8 + count)
            tap = TAPS - 1 - i if mirrored else i
            for k in range(wide):
                columns = pl.ds(pl.multiple_of(first_column + 128 * k, 128), 128)
                part = taps_ref[tap : tap + 1, columns] * source[i % 8, at, columns]
                sums[k] = sums[k] + (jnp.where(mask, part, 0.0) if step else part)
        return sums

    WIDE, TALL = 2, 64

    def convolve(low, tall):
        rows = slice(low, low + tall)

        def one(c):
            sums = over_taps(shift, low, tall, WIDE, c * 128 * WIDE, False)
            for k in range(WIDE):
                columns = pl.ds(pl.multiple_of(c * 128 * WIDE + 128 * k, 128), 128)
                conv = sums[k]
                sigma = 1.0 / (1.0 + jnp.exp(-conv))
                layer_ref[rows, columns] = (stream[rows, columns] + conv * sigma).astype(bf16)
                grad = cot_ref[rows, columns].astype(f32) * sigma * (1.0 + conv * (1.0 - sigma))
                grad = grad.astype(bf16)
                gpad[EDGE + low : EDGE + low + tall, columns] = grad.astype(f32)
                if low == 0:
                    edge_send[2, :, columns] = grad[0:EDGE, :]
                if low + tall == F:
                    edge_send[3, :, columns] = grad[tall - EDGE : tall, :]

        loop(0, D // (128 * WIDE), one)

    convolve(32, 64)
    halo.wait_recv()
    pad[EDGE + F :, :] = edge_recv[0].astype(f32)
    pad[0:EDGE, :] = edge_recv[1].astype(f32)
    shift_rows(pad, shift, 0, 16)
    shift_rows(pad, shift, 128, 152)

    convolve(0, 32)
    convolve(96, 32)
    grad_halo = edges(1)
    grad_halo.start(0)
    grad_halo.start(1)
    stores[0].start()

    shift_rows(gpad, gshift, 16, 128)

    def kernel_rows(c):
        for i in range(TAPS):
            step = i - TAPS // 2
            mask = inside(step, slice(0, F))
            for k in range(WIDE):
                columns = pl.ds(pl.multiple_of(c * 128 * WIDE + 128 * k, 128), 128)
                part = gpad[EDGE : EDGE + F, columns] * shift[i % 8, i // 8 * 8 : i // 8 * 8 + F, columns]
                if step:
                    part = jnp.where(mask, part, 0.0)
                kpart[pl.ds((c * WIDE + k) * 32 + i, 1), :] = jnp.sum(part, axis=0, keepdims=True)

    loop(0, D // (128 * WIDE), kernel_rows)
    grad_halo.wait_recv()
    gpad[EDGE + F :, :] = edge_recv[2].astype(f32)
    gpad[0:EDGE, :] = edge_recv[3].astype(f32)
    shift_rows(gpad, gshift, 0, 16)
    shift_rows(gpad, gshift, 128, 152)

    dots_ref[...] = jnp.zeros((F, 128), f32)

    def convolve_back(c):
        gains = [jnp.zeros((1, 128), f32)] * WIDE
        for low in range(0, F, TALL):
            rows = slice(low, low + TALL)
            sums = over_taps(gshift, low, TALL, WIDE, c * 128 * WIDE, True)
            for k in range(WIDE):
                columns = pl.ds(pl.multiple_of(c * 128 * WIDE + 128 * k, 128), 128)
                unit = normed[rows, columns]
                gains[k] = gains[k] + jnp.sum(sums[k] * unit, axis=0, keepdims=True)
                scaled = sums[k] * gain_ref[:, columns]
                gshaped[rows, columns] = scaled
                dots_ref[rows, :] += scaled * unit
        for k in range(WIDE):
            kpart[pl.ds((c * WIDE + k) * 32 + TAPS, 1), :] = gains[k]

    loop(0, D // (128 * WIDE), convolve_back)
    mean = jnp.sum(dots_ref[...], axis=1, keepdims=True) * (1.0 / D)

    def kpiece(s):
        return pl.ds(pl.multiple_of(s * 24, 8), 24)

    ksum1 = Exchange(flights, *over_seq, lambda to: kpart.at[kpiece(to)], lambda s: krecv.at[s], ksem1)
    ksum1.start()

    def into_stream(c):
        columns = pl.ds(times(c, 256), 256)
        part = gshaped[:, columns] - normed[:, columns] * mean
        grad = (cot_ref[:, columns].astype(f32) + factor * part).astype(bf16)
        gres[:, columns] = grad

    loop(0, D // 256, into_stream)
    stores[1].start()

    give_grad = Exchange(flights, *over_seq, lambda to: send3.at[to], lambda s: recv3.at[s], sem3)

    def into_attn(j):
        grad = dot(gres[...], w_ref[pl.ds(times(j, 256), 256), :], NT).astype(bf16)
        for part in range(4):
            c = slice(64 * part, 64 * part + 64)
            send3[4 * j + part] = jnp.concatenate([grad[0:64, c], grad[64:128, c]], axis=1)

    loop(0, N // 4, into_attn)
    give_grad.start()
    recv3[me] = send3[me]

    def core_copy(j):
        return pltpu.make_async_remote_copy(
            src_ref=core_send.at[j],
            dst_ref=core_recv.at[j],
            send_sem=core_sem.at[0, j],
            recv_sem=core_sem.at[1, j],
            device_id={"dp": dp + 1 - 2 * core},
            device_id_type=MESH,
        )

    to_core = Copies(flights, N // 2, core_copy)

    def project_grad(j):
        pair = attn[core, :, pl.ds(times(j, 128), 128)]
        for c in range(D // 512):
            columns = slice(512 * c, 512 * c + 512)
            grad = dot(pair, gres[:, columns], TN)
            own[j, :, columns] = grad[0:64, :]
            core_send[j, :, columns] = grad[64:128, :].astype(bf16)
        to_core.start(j)

    loop(0, N // 2, project_grad)

    give_grad.wait_recv()

    def widen_grad(i):
        values = recv3[i].astype(f32)
        rot_g[pl.ds(times(i, F), 64), :] = values[:, :64]
        rot_g[pl.ds(pl.multiple_of(i * F + 64, 64), 64), :] = values[:, 64:]

    loop(0, N, widen_grad)
    rot_g[L : L + F, :] = rot_g[0:F, :]

    def turn_grad(i):
        gr[pl.ds(times(i, F), F), :] = rot_g[pl.ds((start + i * F) & (L - 1), F), :].astype(bf16)

    loop(0, N, turn_grad)

    ksum1.wait_recv()
    krecv[me] = kpart[kpiece(me), :]

    def add_up(ref):
        value = ref[0].astype(f32)
        for i in range(1, ref.shape[0]):
            value = value + ref[i].astype(f32)
        return value

    ksum[...] = add_up(krecv)
    ksum2 = Exchange(flights, *over_dp, lambda to: ksum, lambda s: krecv2.at[s], ksem2)
    ksum2.start()
    krecv2[dp] = ksum[...]
    to_core.wait_recv()

    z_first = Exchange(flights, *over_z, lambda to: z_send.at[to], lambda s: z_recv.at[s], z_sem)

    def add_core(k):
        to = rem(z + k, N // 2)
        value = own[to] + core_recv[to].astype(f32)
        own[to, :, 0:SPLIT] = value[:, 0:SPLIT]
        z_send[to] = value[:, SPLIT:].astype(bf16)

        @pl.when(k < N // 2)
        def _():
            z_first.start_to(to)

    loop(1, N // 2 + 1, add_core)
    z_recv[z] = z_send[z]

    def pack_seq(j):
        for b in range(N // 2):
            pair = own[b, pl.ds(times(j, 8), 8), 0:SPLIT]
            for k in range(2):
                two[k, 4 * b : 4 * b + 4, :] = pair[4 * k : 4 * k + 4, :]
        for k in range(2):
            seq_send[2 * j + k] = two[k].astype(bf16)

    loop(0, N // 2, pack_seq)
    seq_first = Exchange(flights, *over_seq, lambda to: seq_send.at[to], lambda s: seq_recv.at[s], seq_sem)
    seq_first.start()
    seq_recv[me] = seq_send[me]

    kv_acc[...] = jnp.zeros((2 * H, L), f32)

    def back(t):
        rows = pl.ds(times(t, TILE), TILE)
        keys = pl.ds(times(t // (BIG // TILE), BIG), BIG)
        grad, weights = gr[rows, :], probs[rows, :]
        drift = dot(grad, vr[keys, :], NT)
        row_dot = jnp.sum(grad.astype(f32) * out_rot[rows, :], axis=1, keepdims=True)
        slope = (weights.astype(f32) * (drift - row_dot)).astype(bf16)
        rot_v[rows, :] = dot(slope, kr[keys, :], NN) * H**-0.5
        kv_acc[0:H, keys] += dot(qr[rows, :], slope, TN)
        kv_acc[H:, keys] += dot(grad, weights, TN)

    loop(0, L // TILE, back)

    ksum2.wait_recv()
    kall[kpiece(me), :] = add_up(krecv2)
    ksum3 = Exchange(flights, *over_seq, lambda to: kall.at[kpiece(me)], lambda s: kall.at[kpiece(s)], ksem3)
    ksum3.start()

    def upright(i):
        rows = pl.ds(times(i, F), F)
        rot_qk[rows, :] = kv_acc[:, rows].T

    loop(0, N, upright)
    rot_qk[L : L + F, :] = rot_qk[0:F, :]
    rot_v[L : L + F, :] = rot_v[0:F, :]
    give_back = Exchange(flights, *over_seq, lambda to: send4.at[to], lambda s: recv4.at[s], sem4)

    def pack_back(i):
        at = (i * F - start) & (L - 1)
        send4[i, 0:F, :] = rot_qk[pl.ds(at, F), :].astype(bf16)
        part = rot_v[pl.ds(at, F), :]
        send4[i, F : F + 64, :] = jnp.concatenate([part[0:64, :], part[64:128, :]], axis=1).astype(bf16)

    def send_back(k):
        to = rem(me + k, N)
        pack_back(to)
        give_back.start_to(to)

    loop(1, N, send_back)
    pack_back(me)
    recv4[me] = send4[me]

    seq_first.wait_recv()
    for c in range(SPLIT // 128):
        value = add_up(seq_recv.at[:, :, 128 * c : 128 * c + 128])
        for b in range(N // 2):
            z_send2[b, 4 * c : 4 * c + 4, :] = value[4 * b : 4 * b + 4, :]
    z_second = Exchange(flights, *over_z, lambda to: z_send2.at[to], lambda s: z_recv2.at[s], z_sem2)
    z_second.start()
    z_recv2[z] = z_send2[z]

    z_first.wait_recv()
    for c in range((D - SPLIT) // 128):
        value = add_up(z_recv.at[:, :, 128 * c : 128 * c + 128])
        for j in range(N):
            seq_send2[j, 4 * c : 4 * c + 4, :] = value[4 * j : 4 * j + 4, :]
    seq_second = Exchange(flights, *over_seq, lambda to: seq_send2.at[to], lambda s: seq_recv2.at[s], seq_sem2)
    seq_second.start()
    seq_recv2[me] = seq_send2[me]

    ksum3.wait_recv()
    for c in range(D // 128):
        columns = slice(128 * c, 128 * c + 128)
        ktaps_ref[:, columns] = kall[32 * c : 32 * c + TAPS, :]
        ggain_ref[:, columns] = kall[32 * c + TAPS : 32 * c + 32, :]

    give_back.wait_recv()

    def unpack(j):
        a, b = recv4[2 * j], recv4[2 * j + 1]
        columns = pl.ds(times(j, 128), 128)
        dk_ref[:, columns] = jnp.concatenate([a[0:F, :64], b[0:F, :64]], axis=1)
        dv_ref[:, columns] = jnp.concatenate([a[0:F, 64:], b[0:F, 64:]], axis=1)
        dq_ref[0:64, columns] = jnp.concatenate([a[F:, :64], b[F:, :64]], axis=1)
        dq_ref[64:128, columns] = jnp.concatenate([a[F:, 64:], b[F:, 64:]], axis=1)

    loop(0, N // 2, unpack)
    for store in stores[2:]:
        store.start()

    z_second.wait_recv()
    value = add_up(z_recv2)
    for c in range(SPLIT // 128):
        wgrad_ref[:, 128 * c : 128 * c + 128] = value[4 * c : 4 * c + 4, :]
    seq_second.wait_recv()
    value = add_up(seq_recv2)
    for c in range((D - SPLIT) // 128):
        wgrad_ref[:, SPLIT + 128 * c : SPLIT + 128 * c + 128] = value[4 * c : 4 * c + 4, :]

    for store in stores:
        store.wait()
    for flight in flights:
        flight.wait_send()


def hand_over(*refs):
    sources, targets, held, sems = refs[:8], refs[8:16], refs[16:23], refs[23]
    loads = [pltpu.make_async_copy(sources[i], held[i], sems.at[0, i]) for i in range(7)]
    stores = [pltpu.make_async_copy(held[i], targets[i], sems.at[1, i]) for i in range(7)]
    for load in loads:
        load.start()
    targets[7][...] = sources[7][0, :]
    for load, store in zip(loads, stores):
        load.wait()
        store.start()
    for store in stores:
        store.wait()


def local(resid, query, key, value, out_weight, conv_kernel, conv_gain, recording_ids, cotangent):
    vmem = pl.BlockSpec(memory_space=pltpu.VMEM)
    hbm = pl.BlockSpec(memory_space=pl.ANY)
    scratch = [
        pltpu.VMEM((F, A), bf16),
        pltpu.VMEM((F, A), bf16),
        pltpu.VMEM((F, A), bf16),
        pltpu.VMEM((TAPS, D), f32),
        pltpu.VMEM((1, D), f32),
        pltpu.VMEM((F, D), bf16),
        pltpu.VMEM((F, A), bf16),
        pltpu.VMEM((F, A), bf16),
        pltpu.VMEM((F, A), bf16),
        pltpu.VMEM((8, 152, D), f32),
        pltpu.VMEM((8, 152, D), f32),
        pltpu.VMEM((N, F, 128), bf16),
        pltpu.VMEM((N, F, 128), bf16),
        pltpu.VMEM((N, 64, 128), bf16),
        pltpu.VMEM((N, 64, 128), bf16),
        pltpu.VMEM((N, 8, 128), i32),
        pltpu.VMEM((L + F, 128), f32),
        pltpu.VMEM((L + F, H), f32),
        pltpu.VMEM((L, H), bf16),
        pltpu.VMEM((L, H), bf16),
        pltpu.VMEM((L, H), bf16),
        pltpu.VMEM((L, BIG), bf16),
        pltpu.VMEM((L + F, H), f32),
        pltpu.VMEM((N, 64, 128), bf16),
        pltpu.VMEM((N, 64, 128), bf16),
        pltpu.VMEM((2, F, A), bf16),
        pltpu.VMEM((A, D), bf16),
        pltpu.VMEM((F, D), bf16),
        pltpu.VMEM((F, D), bf16),
        pltpu.VMEM((F, D), f32),
        pltpu.VMEM((F, D), f32),
        pltpu.VMEM((F + 2 * EDGE, D), f32),
        pltpu.VMEM((F + 2 * EDGE, D), f32),
        pltpu.VMEM((F, D), f32),
        pltpu.VMEM((F, D), bf16),
        pltpu.VMEM((F, 128), i32),
        pltpu.VMEM((F, 128), i32),
        pltpu.VMEM((F, 128), f32),
        pltpu.VMEM((4, EDGE, D), bf16),
        pltpu.VMEM((4, EDGE, D), bf16),
        pltpu.VMEM((N, 64, 128), bf16),
        pltpu.VMEM((N, 64, 128), bf16),
        pltpu.VMEM((N, 192, 128), bf16),
        pltpu.VMEM((N, 192, 128), bf16),
        pltpu.VMEM((L + F, H), f32),
        pltpu.VMEM((L, H), bf16),
        pltpu.VMEM((2 * H, L), f32),
        pltpu.VMEM((2, 32, SPLIT), f32),
        pltpu.VMEM((8, 64, D), f32),
        pltpu.VMEM((8, 64, D), bf16),
        pltpu.VMEM((8, 64, D), bf16),
        pltpu.VMEM((8, 64, D - SPLIT), bf16),
        pltpu.VMEM((8, 64, D - SPLIT), bf16),
        pltpu.VMEM((N, 32, SPLIT), bf16),
        pltpu.VMEM((N, 32, SPLIT), bf16),
        pltpu.VMEM((8, SPLIT // 32, 128), f32),
        pltpu.VMEM((8, SPLIT // 32, 128), f32),
        pltpu.VMEM((N, (D - SPLIT) // 32, 128), f32),
        pltpu.VMEM((N, (D - SPLIT) // 32, 128), f32),
        pltpu.VMEM((384, 128), f32),
        pltpu.VMEM((N, 24, 128), f32),
        pltpu.VMEM((24, 128), f32),
        pltpu.VMEM((N, 24, 128), f32),
        pltpu.VMEM((384, 128), f32),
        pltpu.SemaphoreType.DMA((12,)),
        pltpu.SemaphoreType.DMA((2, N)),
        pltpu.SemaphoreType.DMA((2, N)),
        pltpu.SemaphoreType.DMA((2, N)),
        pltpu.SemaphoreType.DMA((2, N)),
        pltpu.SemaphoreType.DMA((2, N)),
        pltpu.SemaphoreType.DMA((2, N)),
        pltpu.SemaphoreType.DMA((2, 4)),
        pltpu.SemaphoreType.DMA((2, 8)),
        pltpu.SemaphoreType.DMA((2, 8)),
        pltpu.SemaphoreType.DMA((2, N)),
        pltpu.SemaphoreType.DMA((2, 8)),
        pltpu.SemaphoreType.DMA((2, N)),
        pltpu.SemaphoreType.DMA((2, N)),
        pltpu.SemaphoreType.DMA((2, N)),
        pltpu.SemaphoreType.DMA((2, N)),
    ]
    outs = pl.pallas_call(
        kernel,
        out_shape=(
            jax.ShapeDtypeStruct((F, D), bf16),
            jax.ShapeDtypeStruct((F, D), bf16),
            jax.ShapeDtypeStruct((F, A), bf16),
            jax.ShapeDtypeStruct((F, A), bf16),
            jax.ShapeDtypeStruct((F, A), bf16),
            jax.ShapeDtypeStruct((4, D), f32),
            jax.ShapeDtypeStruct((TAPS, D), f32),
            jax.ShapeDtypeStruct((1, D), f32),
        ),
        in_specs=[hbm] * 3 + [vmem, hbm, vmem] + [hbm] * 3,
        out_specs=(hbm,) * 5 + (vmem,) * 3,
        scratch_shapes=scratch,
        compiler_params=pltpu.CompilerParams(
            collective_id=0, has_side_effects=True, vmem_limit_bytes=60 * 1024 * 1024
        ),
        name="conformer",
    )(
        query[0], key[0], value[0], recording_ids, conv_kernel, conv_gain,
        resid[0], cotangent[0], out_weight,
    )
    layer_out, grad_resid, grad_q, grad_k, grad_v, grad_w, grad_taps, grad_gain = pl.pallas_call(
        hand_over,
        out_shape=tuple(jax.ShapeDtypeStruct(out.shape, out.dtype) for out in outs[:7])
        + (jax.ShapeDtypeStruct((D,), f32),),
        in_specs=[hbm] * 7 + [vmem],
        out_specs=(hbm,) * 7 + (vmem,),
        scratch_shapes=[pltpu.VMEM(out.shape, out.dtype) for out in outs[:7]]
        + [pltpu.SemaphoreType.DMA((2, 7))],
        name="hand_over",
    )(*outs)
    return (
        layer_out[None], grad_resid[None], grad_q[None], grad_k[None], grad_v[None],
        grad_w, grad_taps, grad_gain,
    )


def solution(mesh):
    rows = P("dp", "seq", None)
    return jax.shard_map(
        local,
        mesh=mesh,
        in_specs=(rows, rows, rows, rows, P(), P(), P(), P("dp", "seq"), rows),
        out_specs=(rows, rows, rows, rows, rows, P(("dp", "seq"), None), P(), P()),
        check_vma=False,
    )
```

```python
import jax
import jax.numpy as jnp
from jax import lax
from jax.experimental import pallas as pl
from jax.experimental.pallas import tpu as pltpu
from jax.sharding import PartitionSpec as P

EPSILON = 1e-05
N = 16
F = 128
L = 2048
BIG = 1024
H = 64
A = 1024
D = 1536
TAPS = 31
EDGE = 16
TILE = 256
SPLIT = 1024
MESH = pl.DeviceIdType.MESH
f32, bf16, i32 = jnp.float32, jnp.bfloat16, jnp.int32


def rem(value, size):
    return lax.rem(value, size)


def loop(low, high, body):
    def step(i, carry):
        body(i)
        return carry

    lax.fori_loop(low, high, step, 0)


def times(value, size):
    return pl.multiple_of(value * size, size)


def dot(a, b, dims):
    return lax.dot_general(a, b, (dims, ((), ())), preferred_element_type=f32)


NT = ((1,), (1,))
NN = ((1,), (0,))
TN = ((0,), (0,))


class Copies:
    def __init__(self, flights, count, copy):
        self.count, self.copy, self.received = count, copy, False
        flights.append(self)

    def start(self, i):
        self.copy(i).start()

    def wait_recv(self):
        self.received = True
        loop(0, self.count, lambda i: self.copy(i).wait_recv())

    def wait_send(self):
        loop(0, self.count, lambda i: self.copy(i).wait_send())


class Exchange:
    def __init__(self, flights, device, count, me, send, recv, sems):
        self.device, self.count, self.me = device, count, me
        self.send, self.recv, self.sems = send, recv, sems
        self.received = False
        flights.append(self)

    def copy(self, to, slot):
        return pltpu.make_async_remote_copy(
            src_ref=self.send(to),
            dst_ref=self.recv(slot),
            send_sem=self.sems.at[0, to],
            recv_sem=self.sems.at[1, slot],
            device_id=self.device(to),
            device_id_type=MESH,
        )

    def others(self, body):
        loop(1, self.count, lambda k: body(rem(self.me + k, self.count)))

    def start_to(self, to):
        self.copy(to, self.me).start()

    def start(self):
        self.others(self.start_to)

    def wait_recv(self):
        self.received = True
        self.others(lambda source: self.copy(source, source).wait_recv())

    def wait_send(self):
        self.others(lambda to: self.copy(to, self.me).wait_send())


def kernel(
    q_hbm, k_hbm, v_hbm, ids_ref, taps_hbm, gain_in, resid_hbm, cot_hbm, w_hbm,
    layer_ref, gres, dq_ref, dk_ref, dv_ref, wgrad_ref, ktaps_ref, ggain_ref,
    q_ref, k_ref, v_ref, taps_ref, gain_ref, shift, gshift, send0, recv0,
    send1, recv1, ids_all, rot_qk, rot_v, qr, kr, vr, probs, out_rot, send2, recv2, attn,
    w_ref, resid_ref, cot_ref, stream, normed, pad, gpad, gshaped, near_next, near_prev, dots_ref,
    edge_send, edge_recv, send3, recv3, send4, recv4, rot_g, gr, kv_acc,
    two, own, core_send, core_recv, z_send, z_recv, seq_send, seq_recv, z_send2, z_recv2, seq_send2, seq_recv2,
    kpart, krecv, ksum, krecv2, kall,
    local_sem, sem0, sem1, sem_ids, sem2, sem3, sem4, edge_sem, core_sem, z_sem, seq_sem, z_sem2, seq_sem2, ksem1, ksem2, ksem3,
):
    flights = []
    me, dp = lax.axis_index("seq"), lax.axis_index("dp")
    core, z = rem(dp, 2), dp // 2
    over_seq = (lambda to: {"seq": to}), N, me
    over_dp = (lambda to: {"dp": to}), N, dp
    over_z = (lambda to: {"dp": 2 * to + core}), N // 2, z
    pairs = (
        (q_hbm, q_ref), (k_hbm, k_ref), (v_hbm, v_ref),
        (w_hbm, w_ref), (resid_hbm, resid_ref), (cot_hbm, cot_ref), (taps_hbm, taps_ref),
    )
    moves = [pltpu.make_async_copy(a, b, local_sem.at[i]) for i, (a, b) in enumerate(pairs)]
    first, loads = moves[:3], moves[3:]
    for load in first:
        load.start()
    gain_ref[0, :] = gain_in[...]

    barrier = pltpu.get_barrier_semaphore()

    def greet(k):
        pl.semaphore_signal(barrier, inc=1, device_id={"seq": rem(me + k, N)}, device_id_type=MESH)
        pl.semaphore_signal(barrier, inc=1, device_id={"dp": rem(dp + k, N)}, device_id_type=MESH)

    loop(1, N, greet)

    for load in first:
        load.wait()
    for load in loads:
        load.start()

    def pack_qkv(j):
        columns = pl.ds(times(j, 128), 128)
        qp, kp, vp = q_ref[:, columns], k_ref[:, columns], v_ref[:, columns]
        for half in range(2):
            c = slice(64 * half, 64 * half + 64)
            send0[2 * j + half] = jnp.concatenate([qp[:, c], kp[:, c]], axis=1)
            send1[2 * j + half] = jnp.concatenate([vp[0:64, c], vp[64:128, c]], axis=1)

    loop(0, N // 2, pack_qkv)
    ids_all[me] = jnp.broadcast_to(ids_ref[...], (8, F))
    pl.semaphore_wait(barrier, 2 * (N - 1))

    give_ids = Exchange(flights, *over_seq, lambda to: ids_all.at[me], lambda s: ids_all.at[s], sem_ids)
    give_qk = Exchange(flights, *over_seq, lambda to: send0.at[to], lambda s: recv0.at[s], sem0)
    give_v = Exchange(flights, *over_seq, lambda to: send1.at[to], lambda s: recv1.at[s], sem1)
    give_ids.start()
    give_qk.start()
    give_v.start()
    recv0[me] = send0[me]
    recv1[me] = send1[me]
    give_ids.wait_recv()

    ids = ids_all[...]
    bounds = [jnp.int32(0)]
    for u in range(1, 6):
        bounds.append(jnp.sum(jnp.where(ids < u, 1, 0)) // 8)
    bounds.append(jnp.int32(L))
    start = jnp.int32(0)
    for u in range(6):
        start = start + jnp.where(bounds[u + 1] - bounds[u] == BIG, bounds[u], 0)
    marks = [(bounds[u] - start - BIG) & (L - 1) for u in range(6)]

    frame = me * F + lax.broadcasted_iota(i32, (F, 128), 0)
    low, high = jnp.zeros((F, 128), i32), jnp.full((F, 128), L, i32)
    for u in range(1, 6):
        low = jnp.maximum(low, jnp.where(bounds[u] <= frame, bounds[u], 0))
        high = jnp.minimum(high, jnp.where(bounds[u] > frame, bounds[u], L))
    near_next[...] = high - frame
    near_prev[...] = frame - low

    give_qk.wait_recv()

    def widen(i):
        rot_qk[pl.ds(times(i, F), F), :] = recv0[i].astype(f32)

    loop(0, N, widen)
    rot_qk[L : L + F, :] = rot_qk[0:F, :]

    def turn(i):
        rows = pl.ds(times(i, F), F)
        both = rot_qk[pl.ds((start + i * F) & (L - 1), F), :]
        qr[rows, :] = (both[:, :64] * H**-0.5).astype(bf16)
        kr[rows, :] = both[:, 64:].astype(bf16)

    loop(0, N, turn)

    column = lax.broadcasted_iota(i32, (1, BIG), 1)
    column_part = jnp.zeros((1, BIG), i32)
    for mark in marks:
        column_part = column_part + jnp.where(column >= mark, 1, 0)

    def weigh(base, masked):
        def one(t):
            rows = pl.ds(pl.multiple_of(base + t * TILE, TILE), TILE)
            scores = dot(qr[rows, :], kr[base : base + BIG, :], NT)
            if masked:
                row = t * TILE + lax.broadcasted_iota(i32, (TILE, 1), 0)
                row_part = jnp.zeros((TILE, 1), i32)
                for mark in marks:
                    row_part = row_part + jnp.where(row >= mark, 1, 0)
                scores = jnp.where(row_part == column_part, scores, -1e30)
            unnormed = jnp.exp(scores - jnp.max(scores, axis=1, keepdims=True))
            probs[rows, :] = (unnormed * (1.0 / jnp.sum(unnormed, axis=1, keepdims=True))).astype(bf16)

        def two_tiles(t):
            one(2 * t)
            one(2 * t + 1)

        loop(0, BIG // TILE // 2, two_tiles)

    weigh(0, False)
    weigh(BIG, True)

    give_v.wait_recv()

    def widen_v(i):
        values = recv1[i].astype(f32)
        rot_v[pl.ds(times(i, F), 64), :] = values[:, :64]
        rot_v[pl.ds(pl.multiple_of(i * F + 64, 64), 64), :] = values[:, 64:]

    loop(0, N, widen_v)
    rot_v[L : L + F, :] = rot_v[0:F, :]

    def turn_v(i):
        vr[pl.ds(times(i, F), F), :] = rot_v[pl.ds((start + i * F) & (L - 1), F), :].astype(bf16)

    loop(0, N, turn_v)

    def mix(t):
        rows = pl.ds(times(t, TILE), TILE)
        keys = pl.ds(times(t // (BIG // TILE), BIG), BIG)
        out_rot[rows, :] = dot(probs[rows, :], vr[keys, :], NN).astype(bf16).astype(f32)

    loop(0, L // TILE, mix)
    out_rot[L : L + F, :] = out_rot[0:F, :]

    give_out = Exchange(flights, *over_seq, lambda to: send2.at[to], lambda s: recv2.at[s], sem2)

    def pack_out(i):
        part = out_rot[pl.ds((i * F - start) & (L - 1), F), :]
        send2[i] = jnp.concatenate([part[0:64, :], part[64:128, :]], axis=1).astype(bf16)

    def send_out(k):
        to = rem(me + k, N)
        pack_out(to)
        give_out.start_to(to)

    loop(1, N, send_out)
    pack_out(me)
    recv2[me] = send2[me]
    give_out.wait_recv()

    def join(j):
        a, b = recv2[2 * j], recv2[2 * j + 1]
        columns = pl.ds(times(j, 128), 128)
        for k, (first, second) in enumerate(((a, b), (b, a))):
            attn[k, 0:64, columns] = jnp.concatenate([first[:, :64], second[:, :64]], axis=1)
            attn[k, 64:128, columns] = jnp.concatenate([first[:, 64:], second[:, 64:]], axis=1)

    loop(0, N // 2, join)

    for load in loads:
        load.wait()

    def fold(value):
        return sum(value[:, 128 * c : 128 * c + 128] for c in range(value.shape[1] // 128))

    def project(c, squares):
        columns = pl.ds(times(c, 256), 256)
        part = resid_ref[:, columns].astype(f32) + dot(attn[0], w_ref[:, columns], NN)
        stream[:, columns] = part
        return squares + fold(part * part)

    squares = lax.fori_loop(0, D // 256, project, jnp.zeros((F, 128), f32))
    factor = lax.rsqrt(jnp.sum(squares, axis=1, keepdims=True) * (1.0 / D) + EPSILON)

    def norm(c):
        columns = pl.ds(times(c, 256), 256)
        part = stream[:, columns] * factor
        normed[:, columns] = part
        shaped = (part * gain_ref[:, columns]).astype(bf16)
        pad[EDGE : EDGE + F, columns] = shaped.astype(f32)
        edge_send[0, :, columns] = shaped[0:EDGE, :]
        edge_send[1, :, columns] = shaped[F - EDGE : F, :]

    loop(0, D // 256, norm)

    def edges(turn_of):
        def copy(side):
            return pltpu.make_async_remote_copy(
                src_ref=edge_send.at[2 * turn_of + side],
                dst_ref=edge_recv.at[2 * turn_of + side],
                send_sem=edge_sem.at[0, 2 * turn_of + side],
                recv_sem=edge_sem.at[1, 2 * turn_of + side],
                device_id={"seq": rem(me + jnp.where(side == 0, N - 1, 1), N)},
                device_id_type=MESH,
            )

        return Copies(flights, 2, copy)

    halo = edges(0)
    halo.start(0)
    halo.start(1)

    def shift_rows(source, target, low, high):
        def one(c):
            columns = pl.ds(times(c, 128), 128)
            for s in range(8):
                target[s, low:high, columns] = source[low + s + 1 : high + s + 1, columns]

        loop(0, D // 128, one)

    shift_rows(pad, shift, 16, 128)

    def inside(step, rows):
        if step > 0:
            return near_next[rows, :] > step
        return near_prev[rows, :] >= -step

    def over_taps(source, low, count, wide, first_column, mirrored):
        rows = slice(low, low + count)
        sums = [jnp.zeros((count, 128), f32)] * wide
        for i in range(TAPS):
            step = i - TAPS // 2
            mask = inside(step, rows)
            at = slice(low + i // 8 * 8, low + i // 8 * 8 + count)
            tap = TAPS - 1 - i if mirrored else i
            for k in range(wide):
                columns = pl.ds(pl.multiple_of(first_column + 128 * k, 128), 128)
                part = taps_ref[tap : tap + 1, columns] * source[i % 8, at, columns]
                sums[k] = sums[k] + (jnp.where(mask, part, 0.0) if step else part)
        return sums

    WIDE, TALL, EARLY = 2, 64, 2

    def convolve(low, tall):
        rows = slice(low, low + tall)

        def one(c):
            sums = over_taps(shift, low, tall, WIDE, c * 128 * WIDE, False)
            for k in range(WIDE):
                columns = pl.ds(pl.multiple_of(c * 128 * WIDE + 128 * k, 128), 128)
                conv = sums[k]
                sigma = 1.0 / (1.0 + jnp.exp(-conv))
                layer_ref[rows, columns] = (stream[rows, columns] + conv * sigma).astype(bf16)
                grad = cot_ref[rows, columns].astype(f32) * sigma * (1.0 + conv * (1.0 - sigma))
                grad = grad.astype(bf16)
                gpad[EDGE + low : EDGE + low + tall, columns] = grad.astype(f32)
                if low == 0:
                    edge_send[2, :, columns] = grad[0:EDGE, :]
                if low + tall == F:
                    edge_send[3, :, columns] = grad[tall - EDGE : tall, :]

        loop(0, D // (128 * WIDE), one)

    convolve(32, 64)
    halo.wait_recv()
    pad[EDGE + F :, :] = edge_recv[0].astype(f32)
    pad[0:EDGE, :] = edge_recv[1].astype(f32)
    shift_rows(pad, shift, 0, 16)
    shift_rows(pad, shift, 128, 152)

    convolve(0, 32)
    convolve(96, 32)
    grad_halo = edges(1)
    grad_halo.start(0)
    grad_halo.start(1)

    shift_rows(gpad, gshift, 16, 128)

    def kernel_rows(c):
        for i in range(TAPS):
            step = i - TAPS // 2
            mask = inside(step, slice(0, F))
            for k in range(WIDE):
                columns = pl.ds(pl.multiple_of(c * 128 * WIDE + 128 * k, 128), 128)
                part = gpad[EDGE : EDGE + F, columns] * shift[i % 8, i // 8 * 8 : i // 8 * 8 + F, columns]
                if step:
                    part = jnp.where(mask, part, 0.0)
                kpart[pl.ds((c * WIDE + k) * 32 + i, 1), :] = jnp.sum(part, axis=0, keepdims=True)

    loop(0, EARLY, kernel_rows)
    grad_halo.wait_recv()
    gpad[EDGE + F :, :] = edge_recv[2].astype(f32)
    gpad[0:EDGE, :] = edge_recv[3].astype(f32)
    shift_rows(gpad, gshift, 0, 16)
    shift_rows(gpad, gshift, 128, 152)

    dots_ref[...] = jnp.zeros((F, 128), f32)

    def convolve_back(c):
        gains = [jnp.zeros((1, 128), f32)] * WIDE
        for low in range(0, F, TALL):
            rows = slice(low, low + TALL)
            sums = over_taps(gshift, low, TALL, WIDE, c * 128 * WIDE, True)
            for k in range(WIDE):
                columns = pl.ds(pl.multiple_of(c * 128 * WIDE + 128 * k, 128), 128)
                unit = normed[rows, columns]
                gains[k] = gains[k] + jnp.sum(sums[k] * unit, axis=0, keepdims=True)
                scaled = sums[k] * gain_ref[:, columns]
                gshaped[rows, columns] = scaled
                dots_ref[rows, :] += scaled * unit
        for k in range(WIDE):
            kpart[pl.ds((c * WIDE + k) * 32 + TAPS, 1), :] = gains[k]

    loop(0, D // (128 * WIDE), convolve_back)
    mean = jnp.sum(dots_ref[...], axis=1, keepdims=True) * (1.0 / D)

    def into_stream(c):
        columns = pl.ds(times(c, 256), 256)
        part = gshaped[:, columns] - normed[:, columns] * mean
        grad = (cot_ref[:, columns].astype(f32) + factor * part).astype(bf16)
        gres[:, columns] = grad

    loop(0, D // 256, into_stream)

    give_grad = Exchange(flights, *over_seq, lambda to: send3.at[to], lambda s: recv3.at[s], sem3)

    def into_attn(j):
        grad = dot(gres[...], w_ref[pl.ds(times(j, 256), 256), :], NT).astype(bf16)
        for part in range(4):
            c = slice(64 * part, 64 * part + 64)
            send3[4 * j + part] = jnp.concatenate([grad[0:64, c], grad[64:128, c]], axis=1)

    loop(0, N // 4, into_attn)
    give_grad.start()
    recv3[me] = send3[me]

    def core_copy(j):
        return pltpu.make_async_remote_copy(
            src_ref=core_send.at[j],
            dst_ref=core_recv.at[j],
            send_sem=core_sem.at[0, j],
            recv_sem=core_sem.at[1, j],
            device_id={"dp": dp + 1 - 2 * core},
            device_id_type=MESH,
        )

    to_core = Copies(flights, N // 2, core_copy)

    def project_grad(j):
        pair = attn[core, :, pl.ds(times(j, 128), 128)]
        for c in range(D // 512):
            columns = slice(512 * c, 512 * c + 512)
            grad = dot(pair, gres[:, columns], TN)
            own[j, :, columns] = grad[0:64, :]
            core_send[j, :, columns] = grad[64:128, :].astype(bf16)
        to_core.start(j)

    loop(0, N // 2, project_grad)

    loop(EARLY, D // (128 * WIDE), kernel_rows)

    def kpiece(s):
        return pl.ds(pl.multiple_of(s * 24, 8), 24)

    ksum1 = Exchange(flights, *over_seq, lambda to: kpart.at[kpiece(to)], lambda s: krecv.at[s], ksem1)
    ksum1.start()

    give_grad.wait_recv()

    def widen_grad(i):
        values = recv3[i].astype(f32)
        rot_g[pl.ds(times(i, F), 64), :] = values[:, :64]
        rot_g[pl.ds(pl.multiple_of(i * F + 64, 64), 64), :] = values[:, 64:]

    loop(0, N, widen_grad)
    rot_g[L : L + F, :] = rot_g[0:F, :]

    def turn_grad(i):
        gr[pl.ds(times(i, F), F), :] = rot_g[pl.ds((start + i * F) & (L - 1), F), :].astype(bf16)

    loop(0, N, turn_grad)

    def add_up(ref):
        value = ref[0].astype(f32)
        for i in range(1, ref.shape[0]):
            value = value + ref[i].astype(f32)
        return value

    to_core.wait_recv()

    z_first = Exchange(flights, *over_z, lambda to: z_send.at[to], lambda s: z_recv.at[s], z_sem)

    def add_core(k):
        to = rem(z + k, N // 2)
        value = own[to] + core_recv[to].astype(f32)
        own[to, :, 0:SPLIT] = value[:, 0:SPLIT]
        z_send[to] = value[:, SPLIT:].astype(bf16)

        @pl.when(k < N // 2)
        def _():
            z_first.start_to(to)

    loop(1, N // 2 + 1, add_core)
    z_recv[z] = z_send[z]

    def pack_seq(j):
        for b in range(N // 2):
            pair = own[b, pl.ds(times(j, 8), 8), 0:SPLIT]
            for k in range(2):
                two[k, 4 * b : 4 * b + 4, :] = pair[4 * k : 4 * k + 4, :]
        for k in range(2):
            seq_send[2 * j + k] = two[k].astype(bf16)

    loop(0, N // 2, pack_seq)
    seq_first = Exchange(flights, *over_seq, lambda to: seq_send.at[to], lambda s: seq_recv.at[s], seq_sem)
    seq_first.start()
    seq_recv[me] = seq_send[me]

    kv_acc[...] = jnp.zeros((2 * H, L), f32)

    def back(t):
        rows = pl.ds(times(t, TILE), TILE)
        keys = pl.ds(times(t // (BIG // TILE), BIG), BIG)
        grad, weights = gr[rows, :], probs[rows, :]
        drift = dot(grad, vr[keys, :], NT)
        row_dot = jnp.sum(grad.astype(f32) * out_rot[rows, :], axis=1, keepdims=True)
        slope = (weights.astype(f32) * (drift - row_dot)).astype(bf16)
        rot_v[rows, :] = dot(slope, kr[keys, :], NN) * H**-0.5
        kv_acc[0:H, keys] += dot(qr[rows, :], slope, TN)
        kv_acc[H:, keys] += dot(grad, weights, TN)

    loop(0, L // TILE, back)

    ksum1.wait_recv()
    krecv[me] = kpart[kpiece(me), :]

    ksum[...] = add_up(krecv)
    ksum2 = Exchange(flights, *over_dp, lambda to: ksum, lambda s: krecv2.at[s], ksem2)
    ksum2.start()
    krecv2[dp] = ksum[...]

    def upright(i):
        rows = pl.ds(times(i, F), F)
        rot_qk[rows, :] = kv_acc[:, rows].T

    loop(0, N, upright)
    rot_qk[L : L + F, :] = rot_qk[0:F, :]
    rot_v[L : L + F, :] = rot_v[0:F, :]
    give_back = Exchange(flights, *over_seq, lambda to: send4.at[to], lambda s: recv4.at[s], sem4)

    def pack_back(i):
        at = (i * F - start) & (L - 1)
        send4[i, 0:F, :] = rot_qk[pl.ds(at, F), :].astype(bf16)
        part = rot_v[pl.ds(at, F), :]
        send4[i, F : F + 64, :] = jnp.concatenate([part[0:64, :], part[64:128, :]], axis=1).astype(bf16)

    def send_back(k):
        to = rem(me + k, N)
        pack_back(to)
        give_back.start_to(to)

    loop(1, N, send_back)
    pack_back(me)
    recv4[me] = send4[me]

    seq_first.wait_recv()
    for c in range(SPLIT // 128):
        value = add_up(seq_recv.at[:, :, 128 * c : 128 * c + 128])
        for b in range(N // 2):
            z_send2[b, 4 * c : 4 * c + 4, :] = value[4 * b : 4 * b + 4, :]
    z_second = Exchange(flights, *over_z, lambda to: z_send2.at[to], lambda s: z_recv2.at[s], z_sem2)
    z_second.start()
    z_recv2[z] = z_send2[z]

    ksum2.wait_recv()
    kall[kpiece(me), :] = add_up(krecv2)
    ksum3 = Exchange(flights, *over_seq, lambda to: kall.at[kpiece(me)], lambda s: kall.at[kpiece(s)], ksem3)
    ksum3.start()

    z_first.wait_recv()
    for c in range((D - SPLIT) // 128):
        value = add_up(z_recv.at[:, :, 128 * c : 128 * c + 128])
        for j in range(N):
            seq_send2[j, 4 * c : 4 * c + 4, :] = value[4 * j : 4 * j + 4, :]
    seq_second = Exchange(flights, *over_seq, lambda to: seq_send2.at[to], lambda s: seq_recv2.at[s], seq_sem2)
    seq_second.start()
    seq_recv2[me] = seq_send2[me]

    ksum3.wait_recv()
    for c in range(D // 128):
        columns = slice(128 * c, 128 * c + 128)
        ktaps_ref[:, columns] = kall[32 * c : 32 * c + TAPS, :]
        ggain_ref[:, columns] = kall[32 * c + TAPS : 32 * c + 32, :]

    give_back.wait_recv()

    def unpack(j):
        a, b = recv4[2 * j], recv4[2 * j + 1]
        columns = pl.ds(times(j, 128), 128)
        dk_ref[:, columns] = jnp.concatenate([a[0:F, :64], b[0:F, :64]], axis=1)
        dv_ref[:, columns] = jnp.concatenate([a[0:F, 64:], b[0:F, 64:]], axis=1)
        dq_ref[0:64, columns] = jnp.concatenate([a[F:, :64], b[F:, :64]], axis=1)
        dq_ref[64:128, columns] = jnp.concatenate([a[F:, 64:], b[F:, 64:]], axis=1)

    loop(0, N // 2, unpack)

    z_second.wait_recv()
    value = add_up(z_recv2)
    for c in range(SPLIT // 128):
        wgrad_ref[:, 128 * c : 128 * c + 128] = value[4 * c : 4 * c + 4, :]
    seq_second.wait_recv()
    value = add_up(seq_recv2)
    for c in range((D - SPLIT) // 128):
        wgrad_ref[:, SPLIT + 128 * c : SPLIT + 128 * c + 128] = value[4 * c : 4 * c + 4, :]

    for flight in flights:
        flight.wait_send()


def hand_over(*refs):
    sources, targets, sems = refs[:8], refs[8:16], refs[16]
    copies = [pltpu.make_async_copy(sources[i], targets[i], sems.at[i]) for i in range(7)]
    for copy in copies:
        copy.start()
    targets[7][...] = sources[7][0, :]
    for copy in copies:
        copy.wait()


def local(resid, query, key, value, out_weight, conv_kernel, conv_gain, recording_ids, cotangent):
    vmem = pl.BlockSpec(memory_space=pltpu.VMEM)
    hbm = pl.BlockSpec(memory_space=pl.ANY)
    scratch = [
        pltpu.VMEM((F, A), bf16),
        pltpu.VMEM((F, A), bf16),
        pltpu.VMEM((F, A), bf16),
        pltpu.VMEM((TAPS, D), f32),
        pltpu.VMEM((1, D), f32),
        pltpu.VMEM((8, 152, D), f32),
        pltpu.VMEM((8, 152, D), f32),
        pltpu.VMEM((N, F, 128), bf16),
        pltpu.VMEM((N, F, 128), bf16),
        pltpu.VMEM((N, 64, 128), bf16),
        pltpu.VMEM((N, 64, 128), bf16),
        pltpu.VMEM((N, 8, 128), i32),
        pltpu.VMEM((L + F, 128), f32),
        pltpu.VMEM((L + F, H), f32),
        pltpu.VMEM((L, H), bf16),
        pltpu.VMEM((L, H), bf16),
        pltpu.VMEM((L, H), bf16),
        pltpu.VMEM((L, BIG), bf16),
        pltpu.VMEM((L + F, H), f32),
        pltpu.VMEM((N, 64, 128), bf16),
        pltpu.VMEM((N, 64, 128), bf16),
        pltpu.VMEM((2, F, A), bf16),
        pltpu.VMEM((A, D), bf16),
        pltpu.VMEM((F, D), bf16),
        pltpu.VMEM((F, D), bf16),
        pltpu.VMEM((F, D), f32),
        pltpu.VMEM((F, D), f32),
        pltpu.VMEM((F + 2 * EDGE, D), f32),
        pltpu.VMEM((F + 2 * EDGE, D), f32),
        pltpu.VMEM((F, D), f32),
        pltpu.VMEM((F, 128), i32),
        pltpu.VMEM((F, 128), i32),
        pltpu.VMEM((F, 128), f32),
        pltpu.VMEM((4, EDGE, D), bf16),
        pltpu.VMEM((4, EDGE, D), bf16),
        pltpu.VMEM((N, 64, 128), bf16),
        pltpu.VMEM((N, 64, 128), bf16),
        pltpu.VMEM((N, 192, 128), bf16),
        pltpu.VMEM((N, 192, 128), bf16),
        pltpu.VMEM((L + F, H), f32),
        pltpu.VMEM((L, H), bf16),
        pltpu.VMEM((2 * H, L), f32),
        pltpu.VMEM((2, 32, SPLIT), f32),
        pltpu.VMEM((8, 64, D), f32),
        pltpu.VMEM((8, 64, D), bf16),
        pltpu.VMEM((8, 64, D), bf16),
        pltpu.VMEM((8, 64, D - SPLIT), bf16),
        pltpu.VMEM((8, 64, D - SPLIT), bf16),
        pltpu.VMEM((N, 32, SPLIT), bf16),
        pltpu.VMEM((N, 32, SPLIT), bf16),
        pltpu.VMEM((8, SPLIT // 32, 128), f32),
        pltpu.VMEM((8, SPLIT // 32, 128), f32),
        pltpu.VMEM((N, (D - SPLIT) // 32, 128), f32),
        pltpu.VMEM((N, (D - SPLIT) // 32, 128), f32),
        pltpu.VMEM((384, 128), f32),
        pltpu.VMEM((N, 24, 128), f32),
        pltpu.VMEM((24, 128), f32),
        pltpu.VMEM((N, 24, 128), f32),
        pltpu.VMEM((384, 128), f32),
        pltpu.SemaphoreType.DMA((7,)),
        pltpu.SemaphoreType.DMA((2, N)),
        pltpu.SemaphoreType.DMA((2, N)),
        pltpu.SemaphoreType.DMA((2, N)),
        pltpu.SemaphoreType.DMA((2, N)),
        pltpu.SemaphoreType.DMA((2, N)),
        pltpu.SemaphoreType.DMA((2, N)),
        pltpu.SemaphoreType.DMA((2, 4)),
        pltpu.SemaphoreType.DMA((2, 8)),
        pltpu.SemaphoreType.DMA((2, 8)),
        pltpu.SemaphoreType.DMA((2, N)),
        pltpu.SemaphoreType.DMA((2, 8)),
        pltpu.SemaphoreType.DMA((2, N)),
        pltpu.SemaphoreType.DMA((2, N)),
        pltpu.SemaphoreType.DMA((2, N)),
        pltpu.SemaphoreType.DMA((2, N)),
    ]
    outs = pl.pallas_call(
        kernel,
        out_shape=(
            pltpu.VMEM((F, D), bf16),
            pltpu.VMEM((F, D), bf16),
            pltpu.VMEM((F, A), bf16),
            pltpu.VMEM((F, A), bf16),
            pltpu.VMEM((F, A), bf16),
            pltpu.VMEM((4, D), f32),
            pltpu.VMEM((TAPS, D), f32),
            pltpu.VMEM((1, D), f32),
        ),
        in_specs=[hbm] * 3 + [vmem, hbm, vmem] + [hbm] * 3,
        out_specs=(vmem,) * 8,
        scratch_shapes=scratch,
        compiler_params=pltpu.CompilerParams(
            collective_id=0, has_side_effects=True, vmem_limit_bytes=60 * 1024 * 1024
        ),
        name="conformer",
    )(
        query[0], key[0], value[0], recording_ids, conv_kernel, conv_gain,
        resid[0], cotangent[0], out_weight,
    )
    layer_out, grad_resid, grad_q, grad_k, grad_v, grad_w, grad_taps, grad_gain = pl.pallas_call(
        hand_over,
        out_shape=tuple(jax.ShapeDtypeStruct(out.shape, out.dtype) for out in outs[:7])
        + (jax.ShapeDtypeStruct((D,), f32),),
        in_specs=[vmem] * 8,
        out_specs=(hbm,) * 7 + (vmem,),
        scratch_shapes=[pltpu.SemaphoreType.DMA((7,))],
        name="hand_over",
    )(*(pltpu.with_memory_space_constraint(out, pltpu.VMEM) for out in outs))
    return (
        layer_out[None], grad_resid[None], grad_q[None], grad_k[None], grad_v[None],
        grad_w, grad_taps, grad_gain,
    )


def solution(mesh):
    rows = P("dp", "seq", None)
    return jax.shard_map(
        local,
        mesh=mesh,
        in_specs=(rows, rows, rows, rows, P(), P(), P(), P("dp", "seq"), rows),
        out_specs=(rows, rows, rows, rows, rows, P(("dp", "seq"), None), P(), P()),
        check_vma=False,
    )
```

```python
import jax
import jax.numpy as jnp
from jax import lax
from jax.experimental import pallas as pl
from jax.experimental.pallas import tpu as pltpu
from jax.sharding import PartitionSpec as P

EPSILON = 1e-05
N = 16
F = 128
L = 2048
BIG = 1024
H = 64
A = 1024
D = 1536
TAPS = 31
EDGE = 16
TILE = 256
SPLIT = 1024
MESH = pl.DeviceIdType.MESH
f32, bf16, i32 = jnp.float32, jnp.bfloat16, jnp.int32


def rem(value, size):
    return lax.rem(value, size)


def loop(low, high, body):
    def step(i, carry):
        body(i)
        return carry

    lax.fori_loop(low, high, step, 0)


def times(value, size):
    return pl.multiple_of(value * size, size)


def dot(a, b, dims):
    return lax.dot_general(a, b, (dims, ((), ())), preferred_element_type=f32)


NT = ((1,), (1,))
NN = ((1,), (0,))
TN = ((0,), (0,))


class Copies:
    def __init__(self, flights, count, copy):
        self.count, self.copy, self.received = count, copy, False
        flights.append(self)

    def start(self, i):
        self.copy(i).start()

    def wait_recv(self):
        self.received = True
        loop(0, self.count, lambda i: self.copy(i).wait_recv())

    def wait_send(self):
        loop(0, self.count, lambda i: self.copy(i).wait_send())


class Exchange:
    def __init__(self, flights, device, count, me, send, recv, sems):
        self.device, self.count, self.me = device, count, me
        self.send, self.recv, self.sems = send, recv, sems
        self.received = False
        flights.append(self)

    def copy(self, to, slot):
        return pltpu.make_async_remote_copy(
            src_ref=self.send(to),
            dst_ref=self.recv(slot),
            send_sem=self.sems.at[0, to],
            recv_sem=self.sems.at[1, slot],
            device_id=self.device(to),
            device_id_type=MESH,
        )

    def others(self, body):
        loop(1, self.count, lambda k: body(rem(self.me + k, self.count)))

    def start_to(self, to):
        self.copy(to, self.me).start()

    def start(self):
        self.others(self.start_to)

    def wait_recv(self):
        self.received = True
        self.others(lambda source: self.copy(source, source).wait_recv())

    def wait_send(self):
        self.others(lambda to: self.copy(to, self.me).wait_send())


def kernel(
    q_hbm, k_hbm, v_hbm, ids_ref, taps_hbm, gain_in, resid_hbm, cot_hbm, w_hbm,
    layer_ref, gres, dq_ref, dk_ref, dv_ref, wgrad_ref, ktaps_ref, ggain_ref,
    q_ref, k_ref, v_ref, taps_ref, gain_ref, shift, gshift, send0, recv0,
    send1, recv1, ids_all, rot_qk, rot_v, qr, kr, vr, probs, out_rot, send2, recv2, attn,
    w_ref, resid_ref, cot_ref, stream, normed, pad, gpad, gshaped, near_next, near_prev, dots_ref,
    edge_send, edge_recv, send3, recv3, send4, recv4, rot_g, gr, kv_acc,
    two, own, core_send, core_recv, z_send, z_recv, seq_send, seq_recv, z_send2, z_recv2, seq_send2, seq_recv2,
    kpart, krecv, ksum, krecv2, kall,
    local_sem, sem0, sem1, sem_ids, sem2, sem3, sem4, edge_sem, core_sem, z_sem, seq_sem, z_sem2, seq_sem2, ksem1, ksem2, ksem3,
):
    flights = []
    me, dp = lax.axis_index("seq"), lax.axis_index("dp")
    core, z = rem(dp, 2), dp // 2
    over_seq = (lambda to: {"seq": to}), N, me
    over_dp = (lambda to: {"dp": to}), N, dp
    over_z = (lambda to: {"dp": 2 * to + core}), N // 2, z
    pairs = (
        (q_hbm, q_ref), (k_hbm, k_ref), (v_hbm, v_ref),
        (w_hbm, w_ref), (resid_hbm, resid_ref), (cot_hbm, cot_ref), (taps_hbm, taps_ref),
    )
    moves = [pltpu.make_async_copy(a, b, local_sem.at[i]) for i, (a, b) in enumerate(pairs)]
    first, loads = moves[:3], moves[3:]
    for load in first:
        load.start()
    gain_ref[0, :] = gain_in[...]

    barrier = pltpu.get_barrier_semaphore()

    def greet(k):
        pl.semaphore_signal(barrier, inc=1, device_id={"seq": rem(me + k, N)}, device_id_type=MESH)
        pl.semaphore_signal(barrier, inc=1, device_id={"dp": rem(dp + k, N)}, device_id_type=MESH)

    loop(1, N, greet)

    for load in first:
        load.wait()
    for load in loads:
        load.start()

    def pack_qkv(j):
        columns = pl.ds(times(j, 128), 128)
        qp, kp, vp = q_ref[:, columns], k_ref[:, columns], v_ref[:, columns]
        for half in range(2):
            c = slice(64 * half, 64 * half + 64)
            send0[2 * j + half] = jnp.concatenate([qp[:, c], kp[:, c]], axis=1)
            send1[2 * j + half] = jnp.concatenate([vp[0:64, c], vp[64:128, c]], axis=1)

    loop(0, N // 2, pack_qkv)
    ids_all[me] = jnp.broadcast_to(ids_ref[...], (8, F))
    pl.semaphore_wait(barrier, 2 * (N - 1))

    give_ids = Exchange(flights, *over_seq, lambda to: ids_all.at[me], lambda s: ids_all.at[s], sem_ids)
    give_qk = Exchange(flights, *over_seq, lambda to: send0.at[to], lambda s: recv0.at[s], sem0)
    give_v = Exchange(flights, *over_seq, lambda to: send1.at[to], lambda s: recv1.at[s], sem1)
    give_ids.start()
    give_qk.start()
    give_v.start()
    recv0[me] = send0[me]
    recv1[me] = send1[me]
    give_ids.wait_recv()

    ids = ids_all[...]
    bounds = [jnp.int32(0)]
    for u in range(1, 6):
        bounds.append(jnp.sum(jnp.where(ids < u, 1, 0)) // 8)
    bounds.append(jnp.int32(L))
    start = jnp.int32(0)
    for u in range(6):
        start = start + jnp.where(bounds[u + 1] - bounds[u] == BIG, bounds[u], 0)
    marks = [(bounds[u] - start - BIG) & (L - 1) for u in range(6)]

    frame = me * F + lax.broadcasted_iota(i32, (F, 128), 0)
    low, high = jnp.zeros((F, 128), i32), jnp.full((F, 128), L, i32)
    for u in range(1, 6):
        low = jnp.maximum(low, jnp.where(bounds[u] <= frame, bounds[u], 0))
        high = jnp.minimum(high, jnp.where(bounds[u] > frame, bounds[u], L))
    near_next[...] = high - frame
    near_prev[...] = frame - low

    give_qk.wait_recv()

    def widen(i):
        rot_qk[pl.ds(times(i, F), F), :] = recv0[i].astype(f32)

    loop(0, N, widen)
    rot_qk[L : L + F, :] = rot_qk[0:F, :]

    def turn(i):
        rows = pl.ds(times(i, F), F)
        both = rot_qk[pl.ds((start + i * F) & (L - 1), F), :]
        qr[rows, :] = (both[:, :64] * H**-0.5).astype(bf16)
        kr[rows, :] = both[:, 64:].astype(bf16)

    loop(0, N, turn)

    column = lax.broadcasted_iota(i32, (1, BIG), 1)
    column_part = jnp.zeros((1, BIG), i32)
    for mark in marks:
        column_part = column_part + jnp.where(column >= mark, 1, 0)

    def weigh(base, masked):
        def one(t):
            rows = pl.ds(pl.multiple_of(base + t * TILE, TILE), TILE)
            scores = dot(qr[rows, :], kr[base : base + BIG, :], NT)
            if masked:
                row = t * TILE + lax.broadcasted_iota(i32, (TILE, 1), 0)
                row_part = jnp.zeros((TILE, 1), i32)
                for mark in marks:
                    row_part = row_part + jnp.where(row >= mark, 1, 0)
                scores = jnp.where(row_part == column_part, scores, -1e30)
            unnormed = jnp.exp(scores - jnp.max(scores, axis=1, keepdims=True))
            probs[rows, :] = (unnormed * (1.0 / jnp.sum(unnormed, axis=1, keepdims=True))).astype(bf16)

        def two_tiles(t):
            one(2 * t)
            one(2 * t + 1)

        loop(0, BIG // TILE // 2, two_tiles)

    weigh(0, False)
    weigh(BIG, True)

    give_v.wait_recv()

    def widen_v(i):
        values = recv1[i].astype(f32)
        rot_v[pl.ds(times(i, F), 64), :] = values[:, :64]
        rot_v[pl.ds(pl.multiple_of(i * F + 64, 64), 64), :] = values[:, 64:]

    loop(0, N, widen_v)
    rot_v[L : L + F, :] = rot_v[0:F, :]

    def turn_v(i):
        vr[pl.ds(times(i, F), F), :] = rot_v[pl.ds((start + i * F) & (L - 1), F), :].astype(bf16)

    loop(0, N, turn_v)

    def mix(t):
        rows = pl.ds(times(t, TILE), TILE)
        keys = pl.ds(times(t // (BIG // TILE), BIG), BIG)
        out_rot[rows, :] = dot(probs[rows, :], vr[keys, :], NN).astype(bf16).astype(f32)

    loop(0, L // TILE // 2, lambda t: (mix(2 * t), mix(2 * t + 1)))
    out_rot[L : L + F, :] = out_rot[0:F, :]

    give_out = Exchange(flights, *over_seq, lambda to: send2.at[to], lambda s: recv2.at[s], sem2)

    def pack_out(i):
        part = out_rot[pl.ds((i * F - start) & (L - 1), F), :]
        send2[i] = jnp.concatenate([part[0:64, :], part[64:128, :]], axis=1).astype(bf16)

    def send_out(k):
        to = rem(me + k, N)
        pack_out(to)
        give_out.start_to(to)

    loop(1, N, send_out)
    pack_out(me)
    recv2[me] = send2[me]
    give_out.wait_recv()

    def join(j):
        a, b = recv2[2 * j], recv2[2 * j + 1]
        columns = pl.ds(times(j, 128), 128)
        for k, (first, second) in enumerate(((a, b), (b, a))):
            attn[k, 0:64, columns] = jnp.concatenate([first[:, :64], second[:, :64]], axis=1)
            attn[k, 64:128, columns] = jnp.concatenate([first[:, 64:], second[:, 64:]], axis=1)

    loop(0, N // 2, join)

    for load in loads:
        load.wait()

    def fold(value):
        return sum(value[:, 128 * c : 128 * c + 128] for c in range(value.shape[1] // 128))

    def project(c, squares):
        columns = pl.ds(times(c, 256), 256)
        part = resid_ref[:, columns].astype(f32) + dot(attn[0], w_ref[:, columns], NN)
        stream[:, columns] = part
        return squares + fold(part * part)

    squares = lax.fori_loop(0, D // 256, project, jnp.zeros((F, 128), f32))
    factor = lax.rsqrt(jnp.sum(squares, axis=1, keepdims=True) * (1.0 / D) + EPSILON)

    def norm(c):
        columns = pl.ds(times(c, 256), 256)
        part = stream[:, columns] * factor
        normed[:, columns] = part
        shaped = (part * gain_ref[:, columns]).astype(bf16)
        pad[EDGE : EDGE + F, columns] = shaped.astype(f32)
        edge_send[0, :, columns] = shaped[0:EDGE, :]
        edge_send[1, :, columns] = shaped[F - EDGE : F, :]

    loop(0, D // 256, norm)

    def edges(turn_of):
        def copy(side):
            return pltpu.make_async_remote_copy(
                src_ref=edge_send.at[2 * turn_of + side],
                dst_ref=edge_recv.at[2 * turn_of + side],
                send_sem=edge_sem.at[0, 2 * turn_of + side],
                recv_sem=edge_sem.at[1, 2 * turn_of + side],
                device_id={"seq": rem(me + jnp.where(side == 0, N - 1, 1), N)},
                device_id_type=MESH,
            )

        return Copies(flights, 2, copy)

    halo = edges(0)
    halo.start(0)
    halo.start(1)

    def shift_rows(source, target, low, high):
        def one(c):
            columns = pl.ds(times(c, 128), 128)
            for s in range(8):
                target[s, low:high, columns] = source[low + s + 1 : high + s + 1, columns]

        loop(0, D // 128, one)

    shift_rows(pad, shift, 16, 128)

    def inside(step, rows):
        if step > 0:
            return near_next[rows, :] > step
        return near_prev[rows, :] >= -step

    def over_taps(source, low, count, wide, first_column, mirrored):
        rows = slice(low, low + count)
        sums = [jnp.zeros((count, 128), f32)] * wide
        for i in range(TAPS):
            step = i - TAPS // 2
            mask = inside(step, rows)
            at = slice(low + i // 8 * 8, low + i // 8 * 8 + count)
            tap = TAPS - 1 - i if mirrored else i
            for k in range(wide):
                columns = pl.ds(pl.multiple_of(first_column + 128 * k, 128), 128)
                part = taps_ref[tap : tap + 1, columns] * source[i % 8, at, columns]
                sums[k] = sums[k] + (jnp.where(mask, part, 0.0) if step else part)
        return sums

    WIDE, TALL, EARLY = 2, 32, 2

    def convolve(low, tall):
        rows = slice(low, low + tall)

        def one(c):
            sums = over_taps(shift, low, tall, WIDE, c * 128 * WIDE, False)
            for k in range(WIDE):
                columns = pl.ds(pl.multiple_of(c * 128 * WIDE + 128 * k, 128), 128)
                conv = sums[k]
                sigma = 1.0 / (1.0 + jnp.exp(-conv))
                layer_ref[rows, columns] = (stream[rows, columns] + conv * sigma).astype(bf16)
                grad = cot_ref[rows, columns].astype(f32) * sigma * (1.0 + conv * (1.0 - sigma))
                grad = grad.astype(bf16)
                gpad[EDGE + low : EDGE + low + tall, columns] = grad.astype(f32)
                if low == 0:
                    edge_send[2, :, columns] = grad[0:EDGE, :]
                if low + tall == F:
                    edge_send[3, :, columns] = grad[tall - EDGE : tall, :]

        loop(0, D // (128 * WIDE), one)

    convolve(32, 32)
    convolve(64, 32)
    halo.wait_recv()
    pad[EDGE + F :, :] = edge_recv[0].astype(f32)
    pad[0:EDGE, :] = edge_recv[1].astype(f32)
    shift_rows(pad, shift, 0, 16)
    shift_rows(pad, shift, 128, 152)

    convolve(0, 32)
    convolve(96, 32)
    grad_halo = edges(1)
    grad_halo.start(0)
    grad_halo.start(1)

    shift_rows(gpad, gshift, 16, 128)

    def kernel_rows(c):
        for i in range(TAPS):
            step = i - TAPS // 2
            mask = inside(step, slice(0, F))
            for k in range(WIDE):
                columns = pl.ds(pl.multiple_of(c * 128 * WIDE + 128 * k, 128), 128)
                part = gpad[EDGE : EDGE + F, columns] * shift[i % 8, i // 8 * 8 : i // 8 * 8 + F, columns]
                if step:
                    part = jnp.where(mask, part, 0.0)
                kpart[pl.ds((c * WIDE + k) * 32 + i, 1), :] = jnp.sum(part, axis=0, keepdims=True)

    loop(0, EARLY, kernel_rows)
    grad_halo.wait_recv()
    gpad[EDGE + F :, :] = edge_recv[2].astype(f32)
    gpad[0:EDGE, :] = edge_recv[3].astype(f32)
    shift_rows(gpad, gshift, 0, 16)
    shift_rows(gpad, gshift, 128, 152)

    dots_ref[...] = jnp.zeros((F, 128), f32)

    def convolve_back(c):
        gains = [jnp.zeros((1, 128), f32)] * WIDE
        for low in range(0, F, TALL):
            rows = slice(low, low + TALL)
            sums = over_taps(gshift, low, TALL, WIDE, c * 128 * WIDE, True)
            for k in range(WIDE):
                columns = pl.ds(pl.multiple_of(c * 128 * WIDE + 128 * k, 128), 128)
                unit = normed[rows, columns]
                gains[k] = gains[k] + jnp.sum(sums[k] * unit, axis=0, keepdims=True)
                scaled = sums[k] * gain_ref[:, columns]
                gshaped[rows, columns] = scaled
                dots_ref[rows, :] += scaled * unit
        for k in range(WIDE):
            kpart[pl.ds((c * WIDE + k) * 32 + TAPS, 1), :] = gains[k]

    loop(0, D // (128 * WIDE), convolve_back)
    mean = jnp.sum(dots_ref[...], axis=1, keepdims=True) * (1.0 / D)

    def into_stream(c):
        columns = pl.ds(times(c, 256), 256)
        part = gshaped[:, columns] - normed[:, columns] * mean
        grad = (cot_ref[:, columns].astype(f32) + factor * part).astype(bf16)
        gres[:, columns] = grad

    loop(0, D // 256, into_stream)

    give_grad = Exchange(flights, *over_seq, lambda to: send3.at[to], lambda s: recv3.at[s], sem3)

    def into_attn(j):
        grad = dot(gres[...], w_ref[pl.ds(times(j, 256), 256), :], NT).astype(bf16)
        for part in range(4):
            c = slice(64 * part, 64 * part + 64)
            send3[4 * j + part] = jnp.concatenate([grad[0:64, c], grad[64:128, c]], axis=1)

    loop(0, N // 4, into_attn)
    give_grad.start()
    recv3[me] = send3[me]

    def core_copy(j):
        return pltpu.make_async_remote_copy(
            src_ref=core_send.at[j],
            dst_ref=core_recv.at[j],
            send_sem=core_sem.at[0, j],
            recv_sem=core_sem.at[1, j],
            device_id={"dp": dp + 1 - 2 * core},
            device_id_type=MESH,
        )

    to_core = Copies(flights, N // 2, core_copy)

    def project_grad(j):
        pair = attn[core, :, pl.ds(times(j, 128), 128)]
        for c in range(D // 512):
            columns = slice(512 * c, 512 * c + 512)
            grad = dot(pair, gres[:, columns], TN)
            own[j, :, columns] = grad[0:64, :]
            core_send[j, :, columns] = grad[64:128, :].astype(bf16)
        to_core.start(j)

    loop(0, N // 2, project_grad)

    loop(EARLY, D // (128 * WIDE), kernel_rows)

    def kpiece(s):
        return pl.ds(pl.multiple_of(s * 24, 8), 24)

    ksum1 = Exchange(flights, *over_seq, lambda to: kpart.at[kpiece(to)], lambda s: krecv.at[s], ksem1)
    ksum1.start()

    give_grad.wait_recv()

    def widen_grad(i):
        values = recv3[i].astype(f32)
        rot_g[pl.ds(times(i, F), 64), :] = values[:, :64]
        rot_g[pl.ds(pl.multiple_of(i * F + 64, 64), 64), :] = values[:, 64:]

    loop(0, N, widen_grad)
    rot_g[L : L + F, :] = rot_g[0:F, :]

    def turn_grad(i):
        gr[pl.ds(times(i, F), F), :] = rot_g[pl.ds((start + i * F) & (L - 1), F), :].astype(bf16)

    loop(0, N, turn_grad)

    def add_up(ref):
        value = ref[0].astype(f32)
        for i in range(1, ref.shape[0]):
            value = value + ref[i].astype(f32)
        return value

    to_core.wait_recv()

    z_first = Exchange(flights, *over_z, lambda to: z_send.at[to], lambda s: z_recv.at[s], z_sem)

    def add_core(k):
        to = rem(z + k, N // 2)
        value = own[to] + core_recv[to].astype(f32)
        own[to, :, 0:SPLIT] = value[:, 0:SPLIT]
        z_send[to] = value[:, SPLIT:].astype(bf16)

        @pl.when(k < N // 2)
        def _():
            z_first.start_to(to)

    loop(1, N // 2 + 1, add_core)
    z_recv[z] = z_send[z]

    def pack_seq(j):
        for b in range(N // 2):
            pair = own[b, pl.ds(times(j, 8), 8), 0:SPLIT]
            for k in range(2):
                two[k, 4 * b : 4 * b + 4, :] = pair[4 * k : 4 * k + 4, :]
        for k in range(2):
            seq_send[2 * j + k] = two[k].astype(bf16)

    loop(0, N // 2, pack_seq)
    seq_first = Exchange(flights, *over_seq, lambda to: seq_send.at[to], lambda s: seq_recv.at[s], seq_sem)
    seq_first.start()
    seq_recv[me] = seq_send[me]

    kv_acc[...] = jnp.zeros((2 * H, L), f32)

    def back(t):
        rows = pl.ds(times(t, TILE), TILE)
        keys = pl.ds(times(t // (BIG // TILE), BIG), BIG)
        grad, weights = gr[rows, :], probs[rows, :]
        drift = dot(grad, vr[keys, :], NT)
        row_dot = jnp.sum(grad.astype(f32) * out_rot[rows, :], axis=1, keepdims=True)
        slope = (weights.astype(f32) * (drift - row_dot)).astype(bf16)
        rot_v[rows, :] = dot(slope, kr[keys, :], NN) * H**-0.5
        kv_acc[0:H, keys] += dot(qr[rows, :], slope, TN)
        kv_acc[H:, keys] += dot(grad, weights, TN)

    loop(0, L // TILE // 2, lambda t: (back(2 * t), back(2 * t + 1)))

    ksum1.wait_recv()
    krecv[me] = kpart[kpiece(me), :]

    ksum[...] = add_up(krecv)
    ksum2 = Exchange(flights, *over_dp, lambda to: ksum, lambda s: krecv2.at[s], ksem2)
    ksum2.start()
    krecv2[dp] = ksum[...]

    def upright(i):
        rows = pl.ds(times(i, F), F)
        rot_qk[rows, :] = kv_acc[:, rows].T

    loop(0, N, upright)
    rot_qk[L : L + F, :] = rot_qk[0:F, :]
    rot_v[L : L + F, :] = rot_v[0:F, :]
    give_back = Exchange(flights, *over_seq, lambda to: send4.at[to], lambda s: recv4.at[s], sem4)

    def pack_back(i):
        at = (i * F - start) & (L - 1)
        send4[i, 0:F, :] = rot_qk[pl.ds(at, F), :].astype(bf16)
        part = rot_v[pl.ds(at, F), :]
        send4[i, F : F + 64, :] = jnp.concatenate([part[0:64, :], part[64:128, :]], axis=1).astype(bf16)

    def send_back(k):
        to = rem(me + k, N)
        pack_back(to)
        give_back.start_to(to)

    loop(1, N, send_back)
    pack_back(me)
    recv4[me] = send4[me]

    seq_first.wait_recv()
    for c in range(SPLIT // 128):
        value = add_up(seq_recv.at[:, :, 128 * c : 128 * c + 128])
        for b in range(N // 2):
            z_send2[b, 4 * c : 4 * c + 4, :] = value[4 * b : 4 * b + 4, :]
    z_second = Exchange(flights, *over_z, lambda to: z_send2.at[to], lambda s: z_recv2.at[s], z_sem2)
    z_second.start()
    z_recv2[z] = z_send2[z]

    ksum2.wait_recv()
    kall[kpiece(me), :] = add_up(krecv2)
    ksum3 = Exchange(flights, *over_seq, lambda to: kall.at[kpiece(me)], lambda s: kall.at[kpiece(s)], ksem3)
    ksum3.start()

    z_first.wait_recv()
    for c in range((D - SPLIT) // 128):
        value = add_up(z_recv.at[:, :, 128 * c : 128 * c + 128])
        for j in range(N):
            seq_send2[j, 4 * c : 4 * c + 4, :] = value[4 * j : 4 * j + 4, :]
    seq_second = Exchange(flights, *over_seq, lambda to: seq_send2.at[to], lambda s: seq_recv2.at[s], seq_sem2)
    seq_second.start()
    seq_recv2[me] = seq_send2[me]

    ksum3.wait_recv()
    for c in range(D // 128):
        columns = slice(128 * c, 128 * c + 128)
        ktaps_ref[:, columns] = kall[32 * c : 32 * c + TAPS, :]
        ggain_ref[:, columns] = kall[32 * c + TAPS : 32 * c + 32, :]

    give_back.wait_recv()

    def unpack(j):
        a, b = recv4[2 * j], recv4[2 * j + 1]
        columns = pl.ds(times(j, 128), 128)
        dk_ref[:, columns] = jnp.concatenate([a[0:F, :64], b[0:F, :64]], axis=1)
        dv_ref[:, columns] = jnp.concatenate([a[0:F, 64:], b[0:F, 64:]], axis=1)
        dq_ref[0:64, columns] = jnp.concatenate([a[F:, :64], b[F:, :64]], axis=1)
        dq_ref[64:128, columns] = jnp.concatenate([a[F:, 64:], b[F:, 64:]], axis=1)

    loop(0, N // 2, unpack)

    z_second.wait_recv()
    value = add_up(z_recv2)
    for c in range(SPLIT // 128):
        wgrad_ref[:, 128 * c : 128 * c + 128] = value[4 * c : 4 * c + 4, :]
    seq_second.wait_recv()
    value = add_up(seq_recv2)
    for c in range((D - SPLIT) // 128):
        wgrad_ref[:, SPLIT + 128 * c : SPLIT + 128 * c + 128] = value[4 * c : 4 * c + 4, :]

    for flight in flights:
        flight.wait_send()


def hand_over(*refs):
    sources, targets, sems = refs[:8], refs[8:16], refs[16]
    copies = [pltpu.make_async_copy(sources[i], targets[i], sems.at[i]) for i in range(7)]
    for copy in copies:
        copy.start()
    targets[7][...] = sources[7][0, :]
    for copy in copies:
        copy.wait()


def local(resid, query, key, value, out_weight, conv_kernel, conv_gain, recording_ids, cotangent):
    vmem = pl.BlockSpec(memory_space=pltpu.VMEM)
    hbm = pl.BlockSpec(memory_space=pl.ANY)
    scratch = [
        pltpu.VMEM((F, A), bf16),
        pltpu.VMEM((F, A), bf16),
        pltpu.VMEM((F, A), bf16),
        pltpu.VMEM((TAPS, D), f32),
        pltpu.VMEM((1, D), f32),
        pltpu.VMEM((8, 152, D), f32),
        pltpu.VMEM((8, 152, D), f32),
        pltpu.VMEM((N, F, 128), bf16),
        pltpu.VMEM((N, F, 128), bf16),
        pltpu.VMEM((N, 64, 128), bf16),
        pltpu.VMEM((N, 64, 128), bf16),
        pltpu.VMEM((N, 8, 128), i32),
        pltpu.VMEM((L + F, 128), f32),
        pltpu.VMEM((L + F, H), f32),
        pltpu.VMEM((L, H), bf16),
        pltpu.VMEM((L, H), bf16),
        pltpu.VMEM((L, H), bf16),
        pltpu.VMEM((L, BIG), bf16),
        pltpu.VMEM((L + F, H), f32),
        pltpu.VMEM((N, 64, 128), bf16),
        pltpu.VMEM((N, 64, 128), bf16),
        pltpu.VMEM((2, F, A), bf16),
        pltpu.VMEM((A, D), bf16),
        pltpu.VMEM((F, D), bf16),
        pltpu.VMEM((F, D), bf16),
        pltpu.VMEM((F, D), f32),
        pltpu.VMEM((F, D), f32),
        pltpu.VMEM((F + 2 * EDGE, D), f32),
        pltpu.VMEM((F + 2 * EDGE, D), f32),
        pltpu.VMEM((F, D), f32),
        pltpu.VMEM((F, 128), i32),
        pltpu.VMEM((F, 128), i32),
        pltpu.VMEM((F, 128), f32),
        pltpu.VMEM((4, EDGE, D), bf16),
        pltpu.VMEM((4, EDGE, D), bf16),
        pltpu.VMEM((N, 64, 128), bf16),
        pltpu.VMEM((N, 64, 128), bf16),
        pltpu.VMEM((N, 192, 128), bf16),
        pltpu.VMEM((N, 192, 128), bf16),
        pltpu.VMEM((L + F, H), f32),
        pltpu.VMEM((L, H), bf16),
        pltpu.VMEM((2 * H, L), f32),
        pltpu.VMEM((2, 32, SPLIT), f32),
        pltpu.VMEM((8, 64, D), f32),
        pltpu.VMEM((8, 64, D), bf16),
        pltpu.VMEM((8, 64, D), bf16),
        pltpu.VMEM((8, 64, D - SPLIT), bf16),
        pltpu.VMEM((8, 64, D - SPLIT), bf16),
        pltpu.VMEM((N, 32, SPLIT), bf16),
        pltpu.VMEM((N, 32, SPLIT), bf16),
        pltpu.VMEM((8, SPLIT // 32, 128), f32),
        pltpu.VMEM((8, SPLIT // 32, 128), f32),
        pltpu.VMEM((N, (D - SPLIT) // 32, 128), f32),
        pltpu.VMEM((N, (D - SPLIT) // 32, 128), f32),
        pltpu.VMEM((384, 128), f32),
        pltpu.VMEM((N, 24, 128), f32),
        pltpu.VMEM((24, 128), f32),
        pltpu.VMEM((N, 24, 128), f32),
        pltpu.VMEM((384, 128), f32),
        pltpu.SemaphoreType.DMA((7,)),
        pltpu.SemaphoreType.DMA((2, N)),
        pltpu.SemaphoreType.DMA((2, N)),
        pltpu.SemaphoreType.DMA((2, N)),
        pltpu.SemaphoreType.DMA((2, N)),
        pltpu.SemaphoreType.DMA((2, N)),
        pltpu.SemaphoreType.DMA((2, N)),
        pltpu.SemaphoreType.DMA((2, 4)),
        pltpu.SemaphoreType.DMA((2, 8)),
        pltpu.SemaphoreType.DMA((2, 8)),
        pltpu.SemaphoreType.DMA((2, N)),
        pltpu.SemaphoreType.DMA((2, 8)),
        pltpu.SemaphoreType.DMA((2, N)),
        pltpu.SemaphoreType.DMA((2, N)),
        pltpu.SemaphoreType.DMA((2, N)),
        pltpu.SemaphoreType.DMA((2, N)),
    ]
    outs = pl.pallas_call(
        kernel,
        out_shape=(
            pltpu.VMEM((F, D), bf16),
            pltpu.VMEM((F, D), bf16),
            pltpu.VMEM((F, A), bf16),
            pltpu.VMEM((F, A), bf16),
            pltpu.VMEM((F, A), bf16),
            pltpu.VMEM((4, D), f32),
            pltpu.VMEM((TAPS, D), f32),
            pltpu.VMEM((1, D), f32),
        ),
        in_specs=[hbm] * 3 + [vmem, hbm, vmem] + [hbm] * 3,
        out_specs=(vmem,) * 8,
        scratch_shapes=scratch,
        compiler_params=pltpu.CompilerParams(
            collective_id=0, has_side_effects=True, vmem_limit_bytes=60 * 1024 * 1024
        ),
        name="conformer",
    )(
        query[0], key[0], value[0], recording_ids, conv_kernel, conv_gain,
        resid[0], cotangent[0], out_weight,
    )
    layer_out, grad_resid, grad_q, grad_k, grad_v, grad_w, grad_taps, grad_gain = pl.pallas_call(
        hand_over,
        out_shape=tuple(jax.ShapeDtypeStruct(out.shape, out.dtype) for out in outs[:7])
        + (jax.ShapeDtypeStruct((D,), f32),),
        in_specs=[vmem] * 8,
        out_specs=(hbm,) * 7 + (vmem,),
        scratch_shapes=[pltpu.SemaphoreType.DMA((7,))],
        name="hand_over",
    )(*(pltpu.with_memory_space_constraint(out, pltpu.VMEM) for out in outs))
    return (
        layer_out[None], grad_resid[None], grad_q[None], grad_k[None], grad_v[None],
        grad_w, grad_taps, grad_gain,
    )


def solution(mesh):
    rows = P("dp", "seq", None)
    return jax.shard_map(
        local,
        mesh=mesh,
        in_specs=(rows, rows, rows, rows, P(), P(), P(), P("dp", "seq"), rows),
        out_specs=(rows, rows, rows, rows, rows, P(("dp", "seq"), None), P(), P()),
        check_vma=False,
    )
```

```python
import jax
import jax.numpy as jnp
from jax import lax
from jax.experimental import pallas as pl
from jax.experimental.pallas import tpu as pltpu
from jax.sharding import PartitionSpec as P

EPSILON = 1e-05
N = 16
F = 128
L = 2048
BIG = 1024
H = 64
A = 1024
D = 1536
TAPS = 31
EDGE = 16
TILE = 256
SPLIT = 1024
MESH = pl.DeviceIdType.MESH
f32, bf16, i32 = jnp.float32, jnp.bfloat16, jnp.int32


def rem(value, size):
    return lax.rem(value, size)


def loop(low, high, body):
    def step(i, carry):
        body(i)
        return carry

    lax.fori_loop(low, high, step, 0)


def times(value, size):
    return pl.multiple_of(value * size, size)


def loop_by_four(count, body):
    loop(0, count // 4, lambda i: [body(4 * i + k) for k in range(4)])


def dot(a, b, dims):
    return lax.dot_general(a, b, (dims, ((), ())), preferred_element_type=f32)


NT = ((1,), (1,))
NN = ((1,), (0,))
TN = ((0,), (0,))


class Copies:
    def __init__(self, flights, count, copy):
        self.count, self.copy, self.received = count, copy, False
        flights.append(self)

    def start(self, i):
        self.copy(i).start()

    def wait_recv(self):
        self.received = True
        loop(0, self.count, lambda i: self.copy(i).wait_recv())

    def wait_send(self):
        loop(0, self.count, lambda i: self.copy(i).wait_send())


class Exchange:
    def __init__(self, flights, device, count, me, send, recv, sems):
        self.device, self.count, self.me = device, count, me
        self.send, self.recv, self.sems = send, recv, sems
        self.received = False
        flights.append(self)

    def copy(self, to, slot):
        return pltpu.make_async_remote_copy(
            src_ref=self.send(to),
            dst_ref=self.recv(slot),
            send_sem=self.sems.at[0, to],
            recv_sem=self.sems.at[1, slot],
            device_id=self.device(to),
            device_id_type=MESH,
        )

    def others(self, body):
        loop(1, self.count, lambda k: body(rem(self.me + k, self.count)))

    def start_to(self, to):
        self.copy(to, self.me).start()

    def start(self):
        self.others(self.start_to)

    def wait_recv(self):
        self.received = True
        self.others(lambda source: self.copy(source, source).wait_recv())

    def wait_send(self):
        self.others(lambda to: self.copy(to, self.me).wait_send())


def kernel(
    q_hbm, k_hbm, v_hbm, ids_ref, taps_hbm, gain_in, resid_hbm, cot_hbm, w_hbm,
    layer_ref, gres, dq_ref, dk_ref, dv_ref, wgrad_ref, ktaps_ref, ggain_ref,
    q_ref, k_ref, v_ref, taps_ref, gain_ref, shift, gshift, send0, recv0,
    send1, recv1, ids_all, rot_qk, rot_v, qr, kr, vr, probs, out_rot, send2, recv2, attn,
    w_ref, resid_ref, cot_ref, stream, normed, pad, gpad, gshaped, near_next, near_prev, dots_ref,
    edge_send, edge_recv, send3, recv3, send4, recv4, rot_g, gr, kv_acc,
    two, own, core_send, core_recv, z_send, z_recv, seq_send, seq_recv, z_send2, z_recv2, seq_send2, seq_recv2,
    kpart, krecv, ksum, krecv2, kall,
    local_sem, sem0, sem1, sem_ids, sem2, sem3, sem4, edge_sem, core_sem, z_sem, seq_sem, z_sem2, seq_sem2, ksem1, ksem2, ksem3,
):
    flights = []
    me, dp = lax.axis_index("seq"), lax.axis_index("dp")
    core, z = rem(dp, 2), dp // 2
    over_seq = (lambda to: {"seq": to}), N, me
    over_dp = (lambda to: {"dp": to}), N, dp
    over_z = (lambda to: {"dp": 2 * to + core}), N // 2, z
    pairs = (
        (q_hbm, q_ref), (k_hbm, k_ref), (v_hbm, v_ref),
        (w_hbm, w_ref), (resid_hbm, resid_ref), (cot_hbm, cot_ref), (taps_hbm, taps_ref),
    )
    moves = [pltpu.make_async_copy(a, b, local_sem.at[i]) for i, (a, b) in enumerate(pairs)]
    first, loads = moves[:3], moves[3:]
    for load in first:
        load.start()
    gain_ref[0, :] = gain_in[...]

    barrier = pltpu.get_barrier_semaphore()

    def greet(k):
        pl.semaphore_signal(barrier, inc=1, device_id={"seq": rem(me + k, N)}, device_id_type=MESH)
        pl.semaphore_signal(barrier, inc=1, device_id={"dp": rem(dp + k, N)}, device_id_type=MESH)

    loop(1, N, greet)

    for load in first:
        load.wait()
    for load in loads:
        load.start()

    def pack_qkv(j):
        columns = pl.ds(times(j, 128), 128)
        qp, kp, vp = q_ref[:, columns], k_ref[:, columns], v_ref[:, columns]
        for half in range(2):
            c = slice(64 * half, 64 * half + 64)
            send0[2 * j + half] = jnp.concatenate([qp[:, c], kp[:, c]], axis=1)
            send1[2 * j + half] = jnp.concatenate([vp[0:64, c], vp[64:128, c]], axis=1)

    loop(0, N // 2, pack_qkv)
    ids_all[me] = jnp.broadcast_to(ids_ref[...], (8, F))
    pl.semaphore_wait(barrier, 2 * (N - 1))

    give_ids = Exchange(flights, *over_seq, lambda to: ids_all.at[me], lambda s: ids_all.at[s], sem_ids)
    give_qk = Exchange(flights, *over_seq, lambda to: send0.at[to], lambda s: recv0.at[s], sem0)
    give_v = Exchange(flights, *over_seq, lambda to: send1.at[to], lambda s: recv1.at[s], sem1)
    give_ids.start()
    give_qk.start()
    give_v.start()
    recv0[me] = send0[me]
    recv1[me] = send1[me]
    give_ids.wait_recv()

    ids = ids_all[...]
    bounds = [jnp.int32(0)]
    for u in range(1, 6):
        bounds.append(jnp.sum(jnp.where(ids < u, 1, 0)) // 8)
    bounds.append(jnp.int32(L))
    start = jnp.int32(0)
    for u in range(6):
        start = start + jnp.where(bounds[u + 1] - bounds[u] == BIG, bounds[u], 0)
    marks = [(bounds[u] - start - BIG) & (L - 1) for u in range(6)]

    frame = me * F + lax.broadcasted_iota(i32, (F, 128), 0)
    low, high = jnp.zeros((F, 128), i32), jnp.full((F, 128), L, i32)
    for u in range(1, 6):
        low = jnp.maximum(low, jnp.where(bounds[u] <= frame, bounds[u], 0))
        high = jnp.minimum(high, jnp.where(bounds[u] > frame, bounds[u], L))
    near_next[...] = high - frame
    near_prev[...] = frame - low

    give_qk.wait_recv()

    def widen(i):
        rot_qk[pl.ds(times(i, F), F), :] = recv0[i].astype(f32)

    loop_by_four(N, widen)
    rot_qk[L : L + F, :] = rot_qk[0:F, :]

    def turn(i):
        rows = pl.ds(times(i, F), F)
        both = rot_qk[pl.ds((start + i * F) & (L - 1), F), :]
        qr[rows, :] = (both[:, :64] * H**-0.5).astype(bf16)
        kr[rows, :] = both[:, 64:].astype(bf16)

    loop_by_four(N, turn)

    column = lax.broadcasted_iota(i32, (1, BIG), 1)
    column_part = jnp.zeros((1, BIG), i32)
    for mark in marks:
        column_part = column_part + jnp.where(column >= mark, 1, 0)

    def weigh(base, masked):
        def one(t):
            rows = pl.ds(pl.multiple_of(base + t * TILE, TILE), TILE)
            scores = dot(qr[rows, :], kr[base : base + BIG, :], NT)
            if masked:
                row = t * TILE + lax.broadcasted_iota(i32, (TILE, 1), 0)
                row_part = jnp.zeros((TILE, 1), i32)
                for mark in marks:
                    row_part = row_part + jnp.where(row >= mark, 1, 0)
                scores = jnp.where(row_part == column_part, scores, -1e30)
            unnormed = jnp.exp(scores - jnp.max(scores, axis=1, keepdims=True))
            probs[rows, :] = (unnormed * (1.0 / jnp.sum(unnormed, axis=1, keepdims=True))).astype(bf16)

        def two_tiles(t):
            one(2 * t)
            one(2 * t + 1)

        loop(0, BIG // TILE // 2, two_tiles)

    weigh(0, False)
    weigh(BIG, True)

    give_v.wait_recv()

    def widen_v(i):
        values = recv1[i].astype(f32)
        rot_v[pl.ds(times(i, F), 64), :] = values[:, :64]
        rot_v[pl.ds(pl.multiple_of(i * F + 64, 64), 64), :] = values[:, 64:]

    loop_by_four(N, widen_v)
    rot_v[L : L + F, :] = rot_v[0:F, :]

    def turn_v(i):
        vr[pl.ds(times(i, F), F), :] = rot_v[pl.ds((start + i * F) & (L - 1), F), :].astype(bf16)

    loop_by_four(N, turn_v)

    def mix(t):
        rows = pl.ds(times(t, TILE), TILE)
        keys = pl.ds(times(t // (BIG // TILE), BIG), BIG)
        out_rot[rows, :] = dot(probs[rows, :], vr[keys, :], NN).astype(bf16).astype(f32)

    loop(0, L // TILE // 2, lambda t: (mix(2 * t), mix(2 * t + 1)))
    out_rot[L : L + F, :] = out_rot[0:F, :]

    give_out = Exchange(flights, *over_seq, lambda to: send2.at[to], lambda s: recv2.at[s], sem2)

    def pack_out(i):
        part = out_rot[pl.ds((i * F - start) & (L - 1), F), :]
        send2[i] = jnp.concatenate([part[0:64, :], part[64:128, :]], axis=1).astype(bf16)

    def send_out(k):
        to = rem(me + k, N)
        pack_out(to)
        give_out.start_to(to)

    loop(1, N, send_out)
    pack_out(me)
    recv2[me] = send2[me]
    give_out.wait_recv()

    def join(j):
        a, b = recv2[2 * j], recv2[2 * j + 1]
        columns = pl.ds(times(j, 128), 128)
        for k, (first, second) in enumerate(((a, b), (b, a))):
            attn[k, 0:64, columns] = jnp.concatenate([first[:, :64], second[:, :64]], axis=1)
            attn[k, 64:128, columns] = jnp.concatenate([first[:, 64:], second[:, 64:]], axis=1)

    loop(0, N // 2, join)

    for load in loads:
        load.wait()

    def fold(value):
        return sum(value[:, 128 * c : 128 * c + 128] for c in range(value.shape[1] // 128))

    def project(c, squares):
        columns = pl.ds(times(c, 256), 256)
        part = resid_ref[:, columns].astype(f32) + dot(attn[0], w_ref[:, columns], NN)
        stream[:, columns] = part
        return squares + fold(part * part)

    squares = lax.fori_loop(0, D // 256, project, jnp.zeros((F, 128), f32))
    factor = lax.rsqrt(jnp.sum(squares, axis=1, keepdims=True) * (1.0 / D) + EPSILON)

    def norm(c):
        columns = pl.ds(times(c, 256), 256)
        part = stream[:, columns] * factor
        normed[:, columns] = part
        shaped = (part * gain_ref[:, columns]).astype(bf16)
        pad[EDGE : EDGE + F, columns] = shaped.astype(f32)
        edge_send[0, :, columns] = shaped[0:EDGE, :]
        edge_send[1, :, columns] = shaped[F - EDGE : F, :]

    loop(0, D // 256, norm)

    def edges(turn_of):
        def copy(side):
            return pltpu.make_async_remote_copy(
                src_ref=edge_send.at[2 * turn_of + side],
                dst_ref=edge_recv.at[2 * turn_of + side],
                send_sem=edge_sem.at[0, 2 * turn_of + side],
                recv_sem=edge_sem.at[1, 2 * turn_of + side],
                device_id={"seq": rem(me + jnp.where(side == 0, N - 1, 1), N)},
                device_id_type=MESH,
            )

        return Copies(flights, 2, copy)

    halo = edges(0)
    halo.start(0)
    halo.start(1)

    def shift_rows(source, target, low, high):
        def one(c):
            columns = pl.ds(times(c, 128), 128)
            for s in range(8):
                target[s, low:high, columns] = source[low + s + 1 : high + s + 1, columns]

        loop(0, D // 128, one)

    shift_rows(pad, shift, 16, 128)

    def inside(step, rows):
        if step > 0:
            return near_next[rows, :] > step
        return near_prev[rows, :] >= -step

    def over_taps(source, low, count, wide, first_column, mirrored):
        rows = slice(low, low + count)
        sums = [jnp.zeros((count, 128), f32)] * wide
        for i in range(TAPS):
            step = i - TAPS // 2
            mask = inside(step, rows)
            at = slice(low + i // 8 * 8, low + i // 8 * 8 + count)
            tap = TAPS - 1 - i if mirrored else i
            for k in range(wide):
                columns = pl.ds(pl.multiple_of(first_column + 128 * k, 128), 128)
                part = taps_ref[tap : tap + 1, columns] * source[i % 8, at, columns]
                sums[k] = sums[k] + (jnp.where(mask, part, 0.0) if step else part)
        return sums

    WIDE, TALL, EARLY = 2, 32, 2

    def convolve(low, tall):
        rows = slice(low, low + tall)

        def one(c):
            sums = over_taps(shift, low, tall, WIDE, c * 128 * WIDE, False)
            for k in range(WIDE):
                columns = pl.ds(pl.multiple_of(c * 128 * WIDE + 128 * k, 128), 128)
                conv = sums[k]
                sigma = 1.0 / (1.0 + jnp.exp(-conv))
                layer_ref[rows, columns] = (stream[rows, columns] + conv * sigma).astype(bf16)
                grad = cot_ref[rows, columns].astype(f32) * sigma * (1.0 + conv * (1.0 - sigma))
                grad = grad.astype(bf16)
                gpad[EDGE + low : EDGE + low + tall, columns] = grad.astype(f32)
                if low == 0:
                    edge_send[2, :, columns] = grad[0:EDGE, :]
                if low + tall == F:
                    edge_send[3, :, columns] = grad[tall - EDGE : tall, :]

        loop(0, D // (128 * WIDE), one)

    convolve(32, 32)
    convolve(64, 32)
    halo.wait_recv()
    pad[EDGE + F :, :] = edge_recv[0].astype(f32)
    pad[0:EDGE, :] = edge_recv[1].astype(f32)
    shift_rows(pad, shift, 0, 16)
    shift_rows(pad, shift, 128, 152)

    convolve(0, 32)
    convolve(96, 32)
    grad_halo = edges(1)
    grad_halo.start(0)
    grad_halo.start(1)

    shift_rows(gpad, gshift, 16, 128)

    def kernel_rows(c):
        for i in range(TAPS):
            step = i - TAPS // 2
            mask = inside(step, slice(0, F))
            for k in range(WIDE):
                columns = pl.ds(pl.multiple_of(c * 128 * WIDE + 128 * k, 128), 128)
                part = gpad[EDGE : EDGE + F, columns] * shift[i % 8, i // 8 * 8 : i // 8 * 8 + F, columns]
                if step:
                    part = jnp.where(mask, part, 0.0)
                kpart[pl.ds((c * WIDE + k) * 32 + i, 1), :] = jnp.sum(part, axis=0, keepdims=True)

    loop(0, EARLY, kernel_rows)
    grad_halo.wait_recv()
    gpad[EDGE + F :, :] = edge_recv[2].astype(f32)
    gpad[0:EDGE, :] = edge_recv[3].astype(f32)
    shift_rows(gpad, gshift, 0, 16)
    shift_rows(gpad, gshift, 128, 152)

    dots_ref[...] = jnp.zeros((F, 128), f32)

    def convolve_back(c):
        gains = [jnp.zeros((1, 128), f32)] * WIDE
        for low in range(0, F, TALL):
            rows = slice(low, low + TALL)
            sums = over_taps(gshift, low, TALL, WIDE, c * 128 * WIDE, True)
            for k in range(WIDE):
                columns = pl.ds(pl.multiple_of(c * 128 * WIDE + 128 * k, 128), 128)
                unit = normed[rows, columns]
                gains[k] = gains[k] + jnp.sum(sums[k] * unit, axis=0, keepdims=True)
                scaled = sums[k] * gain_ref[:, columns]
                gshaped[rows, columns] = scaled
                dots_ref[rows, :] += scaled * unit
        for k in range(WIDE):
            kpart[pl.ds((c * WIDE + k) * 32 + TAPS, 1), :] = gains[k]

    loop(0, D // (128 * WIDE), convolve_back)
    mean = jnp.sum(dots_ref[...], axis=1, keepdims=True) * (1.0 / D)

    def into_stream(c):
        columns = pl.ds(times(c, 256), 256)
        part = gshaped[:, columns] - normed[:, columns] * mean
        grad = (cot_ref[:, columns].astype(f32) + factor * part).astype(bf16)
        gres[:, columns] = grad

    loop(0, D // 256, into_stream)

    give_grad = Exchange(flights, *over_seq, lambda to: send3.at[to], lambda s: recv3.at[s], sem3)

    def into_attn(j):
        grad = dot(gres[...], w_ref[pl.ds(times(j, 256), 256), :], NT).astype(bf16)
        for part in range(4):
            c = slice(64 * part, 64 * part + 64)
            send3[4 * j + part] = jnp.concatenate([grad[0:64, c], grad[64:128, c]], axis=1)

    loop(0, N // 4, into_attn)
    give_grad.start()
    recv3[me] = send3[me]

    def core_copy(j):
        return pltpu.make_async_remote_copy(
            src_ref=core_send.at[j],
            dst_ref=core_recv.at[j],
            send_sem=core_sem.at[0, j],
            recv_sem=core_sem.at[1, j],
            device_id={"dp": dp + 1 - 2 * core},
            device_id_type=MESH,
        )

    to_core = Copies(flights, N // 2, core_copy)

    def project_grad(j):
        pair = attn[core, :, pl.ds(times(j, 128), 128)]
        for c in range(D // 512):
            columns = slice(512 * c, 512 * c + 512)
            grad = dot(pair, gres[:, columns], TN)
            own[j, :, columns] = grad[0:64, :]
            core_send[j, :, columns] = grad[64:128, :].astype(bf16)
        to_core.start(j)

    loop(0, N // 2, project_grad)

    loop(EARLY, D // (128 * WIDE), kernel_rows)

    def kpiece(s):
        return pl.ds(pl.multiple_of(s * 24, 8), 24)

    ksum1 = Exchange(flights, *over_seq, lambda to: kpart.at[kpiece(to)], lambda s: krecv.at[s], ksem1)
    ksum1.start()

    give_grad.wait_recv()

    def widen_grad(i):
        values = recv3[i].astype(f32)
        rot_g[pl.ds(times(i, F), 64), :] = values[:, :64]
        rot_g[pl.ds(pl.multiple_of(i * F + 64, 64), 64), :] = values[:, 64:]

    loop_by_four(N, widen_grad)
    rot_g[L : L + F, :] = rot_g[0:F, :]

    def turn_grad(i):
        gr[pl.ds(times(i, F), F), :] = rot_g[pl.ds((start + i * F) & (L - 1), F), :].astype(bf16)

    loop_by_four(N, turn_grad)

    def add_up(ref):
        value = ref[0].astype(f32)
        for i in range(1, ref.shape[0]):
            value = value + ref[i].astype(f32)
        return value

    to_core.wait_recv()

    z_first = Exchange(flights, *over_z, lambda to: z_send.at[to], lambda s: z_recv.at[s], z_sem)

    def add_core(k):
        to = rem(z + k, N // 2)
        value = own[to] + core_recv[to].astype(f32)
        own[to, :, 0:SPLIT] = value[:, 0:SPLIT]
        z_send[to] = value[:, SPLIT:].astype(bf16)

        @pl.when(k < N // 2)
        def _():
            z_first.start_to(to)

    loop(1, N // 2 + 1, add_core)
    z_recv[z] = z_send[z]

    def pack_seq(j):
        for b in range(N // 2):
            pair = own[b, pl.ds(times(j, 8), 8), 0:SPLIT]
            for k in range(2):
                two[k, 4 * b : 4 * b + 4, :] = pair[4 * k : 4 * k + 4, :]
        for k in range(2):
            seq_send[2 * j + k] = two[k].astype(bf16)

    loop(0, N // 2, pack_seq)
    seq_first = Exchange(flights, *over_seq, lambda to: seq_send.at[to], lambda s: seq_recv.at[s], seq_sem)
    seq_first.start()
    seq_recv[me] = seq_send[me]

    kv_acc[...] = jnp.zeros((2 * H, L), f32)

    def back(t):
        rows = pl.ds(times(t, TILE), TILE)
        keys = pl.ds(times(t // (BIG // TILE), BIG), BIG)
        grad, weights = gr[rows, :], probs[rows, :]
        drift = dot(grad, vr[keys, :], NT)
        row_dot = jnp.sum(grad.astype(f32) * out_rot[rows, :], axis=1, keepdims=True)
        slope = (weights.astype(f32) * (drift - row_dot)).astype(bf16)
        rot_v[rows, :] = dot(slope, kr[keys, :], NN) * H**-0.5
        kv_acc[0:H, keys] += dot(qr[rows, :], slope, TN)
        kv_acc[H:, keys] += dot(grad, weights, TN)

    loop(0, L // TILE // 2, lambda t: (back(2 * t), back(2 * t + 1)))

    ksum1.wait_recv()
    krecv[me] = kpart[kpiece(me), :]

    ksum[...] = add_up(krecv)
    ksum2 = Exchange(flights, *over_dp, lambda to: ksum, lambda s: krecv2.at[s], ksem2)
    ksum2.start()
    krecv2[dp] = ksum[...]

    def upright(i):
        rows = pl.ds(times(i, F), F)
        rot_qk[rows, :] = kv_acc[:, rows].T

    loop_by_four(N, upright)
    rot_qk[L : L + F, :] = rot_qk[0:F, :]
    rot_v[L : L + F, :] = rot_v[0:F, :]
    give_back = Exchange(flights, *over_seq, lambda to: send4.at[to], lambda s: recv4.at[s], sem4)

    def pack_back(i):
        at = (i * F - start) & (L - 1)
        send4[i, 0:F, :] = rot_qk[pl.ds(at, F), :].astype(bf16)
        part = rot_v[pl.ds(at, F), :]
        send4[i, F : F + 64, :] = jnp.concatenate([part[0:64, :], part[64:128, :]], axis=1).astype(bf16)

    def send_back(k):
        to = rem(me + k, N)
        pack_back(to)
        give_back.start_to(to)

    loop(1, N, send_back)
    pack_back(me)
    recv4[me] = send4[me]

    seq_first.wait_recv()
    for c in range(SPLIT // 128):
        value = add_up(seq_recv.at[:, :, 128 * c : 128 * c + 128])
        for b in range(N // 2):
            z_send2[b, 4 * c : 4 * c + 4, :] = value[4 * b : 4 * b + 4, :]
    z_second = Exchange(flights, *over_z, lambda to: z_send2.at[to], lambda s: z_recv2.at[s], z_sem2)
    z_second.start()
    z_recv2[z] = z_send2[z]

    ksum2.wait_recv()
    kall[kpiece(me), :] = add_up(krecv2)
    ksum3 = Exchange(flights, *over_seq, lambda to: kall.at[kpiece(me)], lambda s: kall.at[kpiece(s)], ksem3)
    ksum3.start()

    z_first.wait_recv()
    for c in range((D - SPLIT) // 128):
        value = add_up(z_recv.at[:, :, 128 * c : 128 * c + 128])
        for j in range(N):
            seq_send2[j, 4 * c : 4 * c + 4, :] = value[4 * j : 4 * j + 4, :]
    seq_second = Exchange(flights, *over_seq, lambda to: seq_send2.at[to], lambda s: seq_recv2.at[s], seq_sem2)
    seq_second.start()
    seq_recv2[me] = seq_send2[me]

    ksum3.wait_recv()
    for c in range(D // 128):
        columns = slice(128 * c, 128 * c + 128)
        ktaps_ref[:, columns] = kall[32 * c : 32 * c + TAPS, :]
        ggain_ref[:, columns] = kall[32 * c + TAPS : 32 * c + 32, :]

    give_back.wait_recv()

    def unpack(j):
        a, b = recv4[2 * j], recv4[2 * j + 1]
        columns = pl.ds(times(j, 128), 128)
        dk_ref[:, columns] = jnp.concatenate([a[0:F, :64], b[0:F, :64]], axis=1)
        dv_ref[:, columns] = jnp.concatenate([a[0:F, 64:], b[0:F, 64:]], axis=1)
        dq_ref[0:64, columns] = jnp.concatenate([a[F:, :64], b[F:, :64]], axis=1)
        dq_ref[64:128, columns] = jnp.concatenate([a[F:, 64:], b[F:, 64:]], axis=1)

    loop(0, N // 2, unpack)

    z_second.wait_recv()
    value = add_up(z_recv2)
    for c in range(SPLIT // 128):
        wgrad_ref[:, 128 * c : 128 * c + 128] = value[4 * c : 4 * c + 4, :]
    seq_second.wait_recv()
    value = add_up(seq_recv2)
    for c in range((D - SPLIT) // 128):
        wgrad_ref[:, SPLIT + 128 * c : SPLIT + 128 * c + 128] = value[4 * c : 4 * c + 4, :]

    for flight in flights:
        flight.wait_send()


def hand_over(*refs):
    sources, targets, sems = refs[:8], refs[8:16], refs[16]
    copies = [pltpu.make_async_copy(sources[i], targets[i], sems.at[i]) for i in range(7)]
    for copy in copies:
        copy.start()
    targets[7][...] = sources[7][0, :]
    for copy in copies:
        copy.wait()


def local(resid, query, key, value, out_weight, conv_kernel, conv_gain, recording_ids, cotangent):
    vmem = pl.BlockSpec(memory_space=pltpu.VMEM)
    hbm = pl.BlockSpec(memory_space=pl.ANY)
    scratch = [
        pltpu.VMEM((F, A), bf16),
        pltpu.VMEM((F, A), bf16),
        pltpu.VMEM((F, A), bf16),
        pltpu.VMEM((TAPS, D), f32),
        pltpu.VMEM((1, D), f32),
        pltpu.VMEM((8, 152, D), f32),
        pltpu.VMEM((8, 152, D), f32),
        pltpu.VMEM((N, F, 128), bf16),
        pltpu.VMEM((N, F, 128), bf16),
        pltpu.VMEM((N, 64, 128), bf16),
        pltpu.VMEM((N, 64, 128), bf16),
        pltpu.VMEM((N, 8, 128), i32),
        pltpu.VMEM((L + F, 128), f32),
        pltpu.VMEM((L + F, H), f32),
        pltpu.VMEM((L, H), bf16),
        pltpu.VMEM((L, H), bf16),
        pltpu.VMEM((L, H), bf16),
        pltpu.VMEM((L, BIG), bf16),
        pltpu.VMEM((L + F, H), f32),
        pltpu.VMEM((N, 64, 128), bf16),
        pltpu.VMEM((N, 64, 128), bf16),
        pltpu.VMEM((2, F, A), bf16),
        pltpu.VMEM((A, D), bf16),
        pltpu.VMEM((F, D), bf16),
        pltpu.VMEM((F, D), bf16),
        pltpu.VMEM((F, D), f32),
        pltpu.VMEM((F, D), f32),
        pltpu.VMEM((F + 2 * EDGE, D), f32),
        pltpu.VMEM((F + 2 * EDGE, D), f32),
        pltpu.VMEM((F, D), f32),
        pltpu.VMEM((F, 128), i32),
        pltpu.VMEM((F, 128), i32),
        pltpu.VMEM((F, 128), f32),
        pltpu.VMEM((4, EDGE, D), bf16),
        pltpu.VMEM((4, EDGE, D), bf16),
        pltpu.VMEM((N, 64, 128), bf16),
        pltpu.VMEM((N, 64, 128), bf16),
        pltpu.VMEM((N, 192, 128), bf16),
        pltpu.VMEM((N, 192, 128), bf16),
        pltpu.VMEM((L + F, H), f32),
        pltpu.VMEM((L, H), bf16),
        pltpu.VMEM((2 * H, L), f32),
        pltpu.VMEM((2, 32, SPLIT), f32),
        pltpu.VMEM((8, 64, D), f32),
        pltpu.VMEM((8, 64, D), bf16),
        pltpu.VMEM((8, 64, D), bf16),
        pltpu.VMEM((8, 64, D - SPLIT), bf16),
        pltpu.VMEM((8, 64, D - SPLIT), bf16),
        pltpu.VMEM((N, 32, SPLIT), bf16),
        pltpu.VMEM((N, 32, SPLIT), bf16),
        pltpu.VMEM((8, SPLIT // 32, 128), f32),
        pltpu.VMEM((8, SPLIT // 32, 128), f32),
        pltpu.VMEM((N, (D - SPLIT) // 32, 128), f32),
        pltpu.VMEM((N, (D - SPLIT) // 32, 128), f32),
        pltpu.VMEM((384, 128), f32),
        pltpu.VMEM((N, 24, 128), f32),
        pltpu.VMEM((24, 128), f32),
        pltpu.VMEM((N, 24, 128), f32),
        pltpu.VMEM((384, 128), f32),
        pltpu.SemaphoreType.DMA((7,)),
        pltpu.SemaphoreType.DMA((2, N)),
        pltpu.SemaphoreType.DMA((2, N)),
        pltpu.SemaphoreType.DMA((2, N)),
        pltpu.SemaphoreType.DMA((2, N)),
        pltpu.SemaphoreType.DMA((2, N)),
        pltpu.SemaphoreType.DMA((2, N)),
        pltpu.SemaphoreType.DMA((2, 4)),
        pltpu.SemaphoreType.DMA((2, 8)),
        pltpu.SemaphoreType.DMA((2, 8)),
        pltpu.SemaphoreType.DMA((2, N)),
        pltpu.SemaphoreType.DMA((2, 8)),
        pltpu.SemaphoreType.DMA((2, N)),
        pltpu.SemaphoreType.DMA((2, N)),
        pltpu.SemaphoreType.DMA((2, N)),
        pltpu.SemaphoreType.DMA((2, N)),
    ]
    outs = pl.pallas_call(
        kernel,
        out_shape=(
            pltpu.VMEM((F, D), bf16),
            pltpu.VMEM((F, D), bf16),
            pltpu.VMEM((F, A), bf16),
            pltpu.VMEM((F, A), bf16),
            pltpu.VMEM((F, A), bf16),
            pltpu.VMEM((4, D), f32),
            pltpu.VMEM((TAPS, D), f32),
            pltpu.VMEM((1, D), f32),
        ),
        in_specs=[hbm] * 3 + [vmem, hbm, vmem] + [hbm] * 3,
        out_specs=(vmem,) * 8,
        scratch_shapes=scratch,
        compiler_params=pltpu.CompilerParams(
            collective_id=0, has_side_effects=True, vmem_limit_bytes=60 * 1024 * 1024
        ),
        name="conformer",
    )(
        query[0], key[0], value[0], recording_ids, conv_kernel, conv_gain,
        resid[0], cotangent[0], out_weight,
    )
    layer_out, grad_resid, grad_q, grad_k, grad_v, grad_w, grad_taps, grad_gain = pl.pallas_call(
        hand_over,
        out_shape=tuple(jax.ShapeDtypeStruct(out.shape, out.dtype) for out in outs[:7])
        + (jax.ShapeDtypeStruct((D,), f32),),
        in_specs=[vmem] * 8,
        out_specs=(hbm,) * 7 + (vmem,),
        scratch_shapes=[pltpu.SemaphoreType.DMA((7,))],
        name="hand_over",
    )(*(pltpu.with_memory_space_constraint(out, pltpu.VMEM) for out in outs))
    return (
        layer_out[None], grad_resid[None], grad_q[None], grad_k[None], grad_v[None],
        grad_w, grad_taps, grad_gain,
    )


def solution(mesh):
    rows = P("dp", "seq", None)
    return jax.shard_map(
        local,
        mesh=mesh,
        in_specs=(rows, rows, rows, rows, P(), P(), P(), P("dp", "seq"), rows),
        out_specs=(rows, rows, rows, rows, rows, P(("dp", "seq"), None), P(), P()),
        check_vma=False,
    )
```
